256 devices in a mesh: seq: 32 (over x, z), ch: 8 (over y, core).
Axes of the slice: x: 4, y: 4, z: 8, core: 2. Of those that a mesh axis runs over, the one named last changes fastest.
Arguments:
- outer_gate: bfloat16 [8192, 4096], P('seq', 'ch'), may hold values from -6 to 6
- inner_gate: bfloat16 [8192, 4096], P('seq', 'ch'), may hold values from -6 to 6
- values: bfloat16 [8192, 4096], P('seq', 'ch'), may hold values from -6 to 6
- filter_taps: float32 [8192, 4096], P('seq', 'ch'), may hold values from -2 to 2, as said below
- skip_scale: float32 [4096], P('ch'), may hold values from 0.5 to 1.5
- out_weight: bfloat16 [4096, 8192], P(None, 'ch'), may hold values from -0.09375 to 0.09375
- out_grad: bfloat16 [8192, 8192], P('seq', 'ch'), may hold values from -6 to 6
Outputs:
- mixed: bfloat16 [8192, 8192], P('seq', 'ch')
- outer_grad: bfloat16 [8192, 4096], P('seq', 'ch')
- inner_grad: bfloat16 [8192, 4096], P('seq', 'ch')
- values_grad: bfloat16 [8192, 4096], P('seq', 'ch')
- taps_grad: float32 [8192, 4096], P('seq', 'ch')
The draws below stay inside these ranges and needn't reach their ends.
Inputs may be any that keep to these rules, and one draw needn't show every extreme that they name: `filter_taps`: taps of each channel's long filter.
All inputs are finite; a program needn't handle non-finite values.
Results may differ from the reference program's by a relative error of at most 0.015.
Values may be sent and summed in bfloat16 or wider, within the bound.
No kernel may reach another device: no remote copies, remote signals or barrier semaphores. Data moves between devices by JAX's collectives and lax.ppermute only.
A program may use at most 128 MiB of HBM per device.

```python
import jax
import jax.numpy as jnp
from jax import lax

D = 8192
CHANNELS = 4096
SEQ_LEN = 8192


def draw_filter_taps(key, part):
    key = jax.random.fold_in(key, 7)
    key_rate, key_taps = jax.random.split(key)
    lags = jnp.arange(SEQ_LEN, dtype=jnp.float32)[:, None]
    spans = jnp.exp(jax.random.uniform(key_rate, (CHANNELS,), jnp.float32, jnp.log(30.0), jnp.log(SEQ_LEN * 4.0)))
    rough = jnp.clip(jax.random.normal(key_taps, (SEQ_LEN, CHANNELS), jnp.float32), -5.0, 5.0)
    scale = jnp.sqrt(1.0 - jnp.exp(-2.0 / spans))
    return rough * jnp.exp(-lags / spans) * scale


def block_scale(rng, dims, pieces, least, top_value):
    gain = 1.0
    for position, parts in pieces:
        heights = jax.random.uniform(jax.random.fold_in(jax.random.fold_in(rng, 6), position), (parts,), jnp.float32, least / len(pieces), top_value / len(pieces))
        gain = gain * jnp.repeat(jnp.exp(heights), dims[position] // parts).reshape((-1,) + (1,) * (len(dims) - 1 - position))
    return gain


def scatter_about(key, dims, width, bound, shards=(), kind=jnp.bfloat16):
    drawn = jax.random.normal(key, dims, jnp.float32) * width
    if len(shards) > 0:
        drawn = block_scale(key, dims, shards, -0.22, 0.18) * drawn
    return jnp.clip(drawn, min=-bound, max=bound).astype(kind)


def setup_inputs(seed: int = 0) -> dict:
    seeds = jax.random.split(jax.random.key(seed), 8)
    outer_gate = scatter_about(seeds[0], (SEQ_LEN, CHANNELS), 1.0, 6.0, ((0, 32), (1, 8)))
    inner_gate = scatter_about(seeds[1], (SEQ_LEN, CHANNELS), 1.0, 6.0, ((0, 32), (1, 8)))
    values = scatter_about(seeds[2], (SEQ_LEN, CHANNELS), 1.0, 6.0, ((0, 32), (1, 8)))
    filter_taps = draw_filter_taps(jax.random.fold_in(seeds[7], 71), 0)
    skip_scale = jnp.clip(0.5 + 1.0 * jax.random.uniform(seeds[4], (CHANNELS,), jnp.float32) ** block_scale(seeds[4], (CHANNELS,), ((0, 8),), -0.2, 0.2), 0.5, 1.5)
    out_weight = scatter_about(seeds[5], (CHANNELS, D), CHANNELS ** -0.5, 0.09375, ((1, 8),))
    out_grad = scatter_about(seeds[6], (SEQ_LEN, D), 1.0, 6.0, ((0, 32), (1, 8)))
    return {"outer_gate": outer_gate, "inner_gate": inner_gate, "values": values, "filter_taps": filter_taps, "skip_scale": skip_scale, "out_weight": out_weight, "out_grad": out_grad}


def spectral_block(blocks):
    signal, taps, grad_signal = blocks
    padded_length = 2 * SEQ_LEN
    signal_spec = jnp.fft.rfft(signal, n=padded_length, axis=0)
    taps_spec = jnp.fft.rfft(taps, n=padded_length, axis=0)
    grad_spec = jnp.fft.rfft(grad_signal, n=padded_length, axis=0)
    conv = jnp.fft.irfft(signal_spec * taps_spec, n=padded_length, axis=0)[:SEQ_LEN]
    corr = jnp.fft.irfft(jnp.conj(taps_spec) * grad_spec, n=padded_length, axis=0)[:SEQ_LEN]
    taps_grad = jnp.fft.irfft(jnp.conj(signal_spec) * grad_spec, n=padded_length, axis=0)[:SEQ_LEN]
    return conv.astype(jnp.float32), corr.astype(jnp.float32), taps_grad.astype(jnp.float32)


def to_blocks(array):
    return array.reshape(SEQ_LEN, CHANNELS // 128, 128).transpose(1, 0, 2)


def from_blocks(array):
    return array.transpose(1, 0, 2).reshape(SEQ_LEN, CHANNELS)


def reference(outer_gate, inner_gate, values, filter_taps, skip_scale, out_weight, out_grad):
    outer = outer_gate.astype(jnp.float32)
    inner = inner_gate.astype(jnp.float32)
    value_f = values.astype(jnp.float32)
    inner_product = inner * value_f
    hidden_grad = jnp.dot(out_grad, out_weight.T, preferred_element_type=jnp.float32)
    signal_grad = hidden_grad * outer
    conv, corr, taps_grad = lax.map(spectral_block, (to_blocks(inner_product), to_blocks(filter_taps), to_blocks(signal_grad)))
    conv = from_blocks(conv)
    corr = from_blocks(corr)
    taps_grad = from_blocks(taps_grad)
    mixed_pre = conv + skip_scale * inner_product
    hidden = (outer * mixed_pre).astype(jnp.bfloat16)
    mixed = jnp.dot(hidden, out_weight, preferred_element_type=jnp.float32).astype(jnp.bfloat16)
    outer_grad = (hidden_grad * mixed_pre).astype(jnp.bfloat16)
    inner_total = corr + skip_scale * signal_grad
    inner_grad = (inner_total * value_f).astype(jnp.bfloat16)
    values_grad = (inner_total * inner).astype(jnp.bfloat16)
    return mixed, outer_grad, inner_grad, values_grad, taps_grad
```

```python
import math

import jax
import jax.numpy as jnp
import numpy as np
from jax import lax
from jax.experimental import pallas as pl
from jax.experimental.pallas import tpu as pltpu
from jax.sharding import PartitionSpec as P

SEQ_PARTS = 32
ROWS = 256
WIDTH = 512
LANE_CH = WIDTH // SEQ_PARTS
COLUMNS = 1024
SLOTS = 32
PADDED = 2 * SEQ_PARTS * ROWS
VMEM_LIMIT = 48 * 1024 * 1024


def transform_tables():
    q = np.arange(SLOTS) + 0.5
    p = np.arange(SEQ_PARTS)
    r = np.arange(ROWS)
    coarse = 2.0 * math.pi * np.outer(q, p) / (2 * SEQ_PARTS)
    eye = np.eye(LANE_CH)
    gather = np.concatenate([np.kron(np.cos(coarse), eye), np.kron(-np.sin(coarse), eye)], 0)
    spread = gather.T * (2.0 / PADDED)
    fine = 2.0 * math.pi * (np.outer(r, r) % ROWS) / ROWS
    cos, sin = np.cos(fine), np.sin(fine)
    turn = np.block([[cos, -sin], [sin, cos]])
    twist = 2.0 * math.pi * np.outer(q, r) / PADDED
    twist = np.repeat(twist, LANE_CH, 0)

    def half(a):
        return jnp.asarray(a, jnp.float32).astype(jnp.bfloat16)

    return (
        half(gather),
        half(spread),
        half(turn),
        jnp.asarray(np.cos(twist), jnp.float32),
        jnp.asarray(np.sin(twist), jnp.float32),
    )


def dot(a, b, contract=((1,), (0,))):
    return lax.dot_general(a, b, (contract, ((), ())), preferred_element_type=jnp.float32)


def bf16(a):
    return a.astype(jnp.bfloat16)


def forward(x, gather, turn, cos, sin):
    count = SLOTS * LANE_CH
    a = dot(gather[...], x)
    real, imag = a[:count], a[count:]
    c, s = cos[...], sin[...]
    b = jnp.concatenate([bf16(real * c + imag * s), bf16(imag * c - real * s)], 1)
    spec = dot(b, turn[...])
    return spec[:, :ROWS], spec[:, ROWS:]


def inverse(real, imag, spread, turn, cos, sin):
    y = jnp.concatenate([bf16(real), bf16(imag)], 1)
    z = dot(y, turn[...], ((1,), (1,)))
    real, imag = z[:, :ROWS], z[:, ROWS:]
    c, s = cos[...], sin[...]
    b = jnp.concatenate([bf16(real * c - imag * s), bf16(imag * c + real * s)], 0)
    return dot(spread[...], b)


def chunks(a):
    return bf16(a).reshape(SEQ_PARTS, LANE_CH, ROWS)


def flat(a):
    return a.reshape(WIDTH, ROWS)


def prepare_kernel(inner, values, taps, out):
    product = inner[...].astype(jnp.float32) * values[...].astype(jnp.float32)
    out[:, :LANE_CH, :] = chunks(product.T)
    out[:, LANE_CH:, :] = chunks(taps[...].T)


def gates_kernel(inner, values, outer, skip, outer_t, outer_skip_t, skip_product_t):
    product = inner[...].astype(jnp.float32) * values[...].astype(jnp.float32)
    out = outer[...].astype(jnp.float32)
    scale = skip[...]
    outer_t[...] = bf16(out.T)
    outer_skip_t[...] = (out * scale).T
    skip_product_t[...] = (product * scale).T


def project_kernel(order, weight, grad, out):
    out[...] = bf16(dot(weight[...], grad[...], ((1,), (1,))))


def project_add_kernel(order, weight, grad, other, out0, out1, out2, out3):
    step = pl.program_id(0)
    total = bf16(dot(weight[...], grad[...], ((1,), (1,))) + other[...].astype(jnp.float32))
    for i, out in enumerate((out0, out1, out2, out3)):

        @pl.when(step == i)
        def _():
            out[...] = total


def first_kernel(got, gather, spread, turn, cos, sin, conv, sr, si, tr, ti):
    x_real, x_imag = forward(flat(got[:, :LANE_CH, :]), gather, turn, cos, sin)
    sr[...] = x_real
    si[...] = x_imag
    t_real, t_imag = forward(flat(got[:, LANE_CH:, :]), gather, turn, cos, sin)
    tr[...] = t_real
    ti[...] = t_imag
    y = inverse(
        x_real * t_real - x_imag * t_imag, x_real * t_imag + x_imag * t_real, spread, turn, cos, sin
    )
    conv[...] = chunks(y)


def middle_kernel(own, a, b, c, outer_t, outer_skip_t, conv, out, hidden_grad_t, skip_grad_t):
    total = (own[...].astype(jnp.float32) + a[...].astype(jnp.float32)) + (
        b[...].astype(jnp.float32) + c[...].astype(jnp.float32)
    )
    hidden_grad_t[...] = total
    skip_grad_t[...] = total * outer_skip_t[...]
    out[:, :LANE_CH, :] = chunks(total * outer_t[...].astype(jnp.float32))
    out[:, LANE_CH:, :] = conv[...]


def second_kernel(got, sr, si, tr, ti, gather, spread, turn, cos, sin, out):
    g_real, g_imag = forward(flat(got[:, :LANE_CH, :]), gather, turn, cos, sin)
    t_real, t_imag = tr[...], ti[...]
    corr = inverse(
        t_real * g_real + t_imag * g_imag, t_real * g_imag - t_imag * g_real, spread, turn, cos, sin
    )
    out[:, :LANE_CH, :] = chunks(corr)
    x_real, x_imag = sr[...], si[...]
    lag = inverse(
        x_real * g_real + x_imag * g_imag, x_real * g_imag - x_imag * g_real, spread, turn, cos, sin
    )
    out[:, LANE_CH:, :] = chunks(lag)


def mix_kernel(got, skip_product_t, outer_t, hidden_grad_t, hidden_t, outer_grad):
    mixed_pre = flat(got[:, LANE_CH:, :]).astype(jnp.float32) + skip_product_t[...]
    hidden_t[...] = bf16(outer_t[...].astype(jnp.float32) * mixed_pre)
    outer_grad[...] = bf16((hidden_grad_t[...] * mixed_pre).T)


def final_kernel(got, skip_grad_t, inner, values, inner_grad, values_grad, taps_grad):
    total = (flat(got[:, :LANE_CH, :]).astype(jnp.float32) + skip_grad_t[...]).T
    inner_grad[...] = bf16(total * values[...].astype(jnp.float32))
    values_grad[...] = bf16(total * inner[...].astype(jnp.float32))
    taps_grad[...] = flat(got[:, LANE_CH:, :]).astype(jnp.float32).T


def blocks_kernel(n, has_base, last, order, *refs):
    parts = refs[:n]
    weight = refs[n]
    out = refs[-2]
    total = refs[-1]
    step = pl.program_id(0)

    @pl.when(step == 0)
    def _():
        total[...] = refs[n + 1][...] if has_base else jnp.zeros_like(total)

    for i in range(n):

        @pl.when(step == i)
        def _():
            total[...] += dot(parts[i][...], weight[...], ((0,), (0,)))

    @pl.when(step == n - 1)
    def _():
        out[...] = total[...].astype(out.dtype)


def shape(dims, dtype):
    return jax.ShapeDtypeStruct(dims, dtype)


def local(kernel, outs, *args, flops=0):
    moved = sum(math.prod(a.shape) * a.dtype.itemsize for a in (*args, *outs))
    return pl.pallas_call(
        kernel,
        out_shape=outs,
        in_specs=[pl.BlockSpec(memory_space=pltpu.VMEM)] * len(args),
        out_specs=tuple(pl.BlockSpec(memory_space=pltpu.VMEM) for _ in outs),
        compiler_params=pltpu.CompilerParams(vmem_limit_bytes=VMEM_LIMIT),
        cost_estimate=pl.CostEstimate(flops=flops, bytes_accessed=moved, transcendentals=0),
    )(*args)


def project(order, weight, grad, other=None):
    block = pl.BlockSpec((WIDTH, ROWS), lambda i, o: (i, 0))
    whole = pl.BlockSpec((WIDTH, ROWS), lambda i, o: (0, 0))
    specs = [
        pl.BlockSpec((WIDTH, COLUMNS), lambda i, o: (o[i], 0)),
        pl.BlockSpec((ROWS, COLUMNS), lambda i, o: (0, 0)),
    ]
    if other is None:
        kernel, outs, out_specs = project_kernel, shape((4 * WIDTH, ROWS), jnp.bfloat16), block
        args = (order, weight, grad)
    else:
        kernel = project_add_kernel
        outs = (shape((WIDTH, ROWS), jnp.bfloat16),) * 4
        out_specs = (whole,) * 4
        specs.append(block)
        args = (order, weight, grad, other)
    return pl.pallas_call(
        kernel,
        out_shape=outs,
        grid_spec=pltpu.PrefetchScalarGridSpec(
            num_scalar_prefetch=1, grid=(4,), in_specs=specs, out_specs=out_specs
        ),
        compiler_params=pltpu.CompilerParams(vmem_limit_bytes=VMEM_LIMIT),
        cost_estimate=pl.CostEstimate(
            flops=2 * 4 * WIDTH * ROWS * COLUMNS, bytes_accessed=6 << 20, transcendentals=0
        ),
    )(*args)


def blocks(order, parts, weight, base=None):
    n = len(parts)
    last = base is not None
    specs = [pl.BlockSpec((WIDTH, ROWS), lambda i, o: (0, 0))] * n
    specs.append(pl.BlockSpec((WIDTH, COLUMNS), lambda i, o: (o[i], 0)))
    args = (order, *parts, weight)
    if last:
        specs.append(pl.BlockSpec((ROWS, COLUMNS), lambda i, o: (0, 0)))
        args = (*args, base)

    def kernel(*refs):
        blocks_kernel(n, last, last, *refs)

    return pl.pallas_call(
        kernel,
        out_shape=shape((ROWS, COLUMNS), jnp.bfloat16 if last else jnp.float32),
        grid_spec=pltpu.PrefetchScalarGridSpec(
            num_scalar_prefetch=1,
            grid=(n,),
            in_specs=specs,
            out_specs=pl.BlockSpec((ROWS, COLUMNS), lambda i, o: (0, 0)),
            scratch_shapes=[pltpu.VMEM((ROWS, COLUMNS), jnp.float32)],
        ),
        compiler_params=pltpu.CompilerParams(vmem_limit_bytes=VMEM_LIMIT),
        cost_estimate=pl.CostEstimate(
            flops=2 * n * WIDTH * ROWS * COLUMNS, bytes_accessed=(n + 2) << 20, transcendentals=0
        ),
    )(*args)


def exchange(a):
    return lax.all_to_all(a, "seq", split_axis=0, concat_axis=0, tiled=True)


def to_partner(a):
    return lax.ppermute(a, "ch", [(i, i ^ 1) for i in range(8)])


def along(a, shift):
    return lax.ppermute(a, "ch", [(i, (i + 2 * shift) % 8) for i in range(8)])


def on_device(outer_gate, inner_gate, values, filter_taps, skip_scale, out_weight, out_grad):
    tables = transform_tables()
    me = lax.axis_index("ch").astype(jnp.int32)
    row, core = me // 2, me % 2
    steps = jnp.arange(4, dtype=jnp.int32)
    ahead = 2 * ((row + steps) % 4)
    behind = 2 * ((row - steps + 4) % 4)
    pass_flops = 2 * 1024 * 512 * 256

    sent = local(
        prepare_kernel, (shape((SEQ_PARTS, 2 * LANE_CH, ROWS), jnp.bfloat16),), inner_gate, values, filter_taps
    )[0]
    got = exchange(sent)

    given = project(ahead + (1 - core), out_weight, out_grad)
    own = project(ahead + core, out_weight, out_grad, to_partner(given))
    sums = [own[0], along(own[2], 2), along(own[1], 1), along(own[3], 3)]

    full = shape((WIDTH, ROWS), jnp.float32)
    outer_t, outer_skip_t, skip_product_t = local(
        gates_kernel,
        (shape((WIDTH, ROWS), jnp.bfloat16), full, full),
        inner_gate,
        values,
        outer_gate,
        skip_scale.reshape(1, WIDTH),
    )
    spectrum = shape((SLOTS * LANE_CH, ROWS), jnp.float32)
    conv, *spectra = local(
        first_kernel,
        (shape((SEQ_PARTS, LANE_CH, ROWS), jnp.bfloat16),) + (spectrum,) * 4,
        got,
        *tables,
        flops=6 * pass_flops,
    )
    sent, hidden_grad_t, skip_grad_t = local(
        middle_kernel,
        (shape((SEQ_PARTS, 2 * LANE_CH, ROWS), jnp.bfloat16), full, full),
        *sums,
        outer_t,
        outer_skip_t,
        conv,
    )
    got = exchange(sent)
    sent = local(
        second_kernel,
        (shape((SEQ_PARTS, 2 * LANE_CH, ROWS), jnp.bfloat16),),
        got,
        *spectra,
        *tables,
        flops=6 * pass_flops,
    )[0]
    returned = exchange(sent)
    hidden_t, outer_grad = local(
        mix_kernel,
        (shape((WIDTH, ROWS), jnp.bfloat16), shape((ROWS, WIDTH), jnp.bfloat16)),
        got,
        skip_product_t,
        outer_t,
        hidden_grad_t,
    )
    near = [hidden_t, along(hidden_t, 1), along(hidden_t, 2), along(hidden_t, 3)]
    far = [to_partner(a) for a in near]
    near_order = jnp.concatenate([behind + core, behind[:1] + (1 - core)])
    part = blocks(near_order, near + far[:1], out_weight)
    mixed = blocks(behind[1:] + (1 - core), far[1:], out_weight, part)
    inner_grad, values_grad, taps_grad = local(
        final_kernel,
        (
            shape((ROWS, WIDTH), jnp.bfloat16),
            shape((ROWS, WIDTH), jnp.bfloat16),
            shape((ROWS, WIDTH), jnp.float32),
        ),
        returned,
        skip_grad_t,
        inner_gate,
        values,
    )
    return (mixed, outer_grad, inner_grad, values_grad, taps_grad)


def solution(mesh):
    placed = (
        P("seq", "ch"),
        P("seq", "ch"),
        P("seq", "ch"),
        P("seq", "ch"),
        P("ch"),
        P(None, "ch"),
        P("seq", "ch"),
    )
    return jax.shard_map(
        on_device,
        mesh=mesh,
        in_specs=placed,
        out_specs=(P("seq", "ch"), P("seq", "ch"), P("seq", "ch"), P("seq", "ch"), P("seq", "ch")),
        check_vma=False,
    )
```

```python
import math

import jax
import jax.numpy as jnp
import numpy as np
from jax import lax
from jax.experimental import pallas as pl
from jax.experimental.pallas import tpu as pltpu
from jax.sharding import PartitionSpec as P

SEQ_PARTS = 32
ROWS = 256
WIDTH = 512
LANE_CH = WIDTH // SEQ_PARTS
COLUMNS = 1024
SLOTS = 32
PADDED = 2 * SEQ_PARTS * ROWS
AHEAD = 3
COSTS = (0.0, 10.0, 2.0, 10.0, 2.0, 1.0, 10.0)


def transform_tables():
    q = np.arange(SLOTS) + 0.5
    p = np.arange(SEQ_PARTS)
    r = np.arange(ROWS)
    coarse = 2.0 * math.pi * np.outer(q, p) / (2 * SEQ_PARTS)
    eye = np.eye(LANE_CH)
    gather = np.concatenate([np.kron(np.cos(coarse), eye), np.kron(-np.sin(coarse), eye)], 0)
    spread = gather.T * (2.0 / PADDED)
    fine = 2.0 * math.pi * (np.outer(r, r) % ROWS) / ROWS
    cos, sin = np.cos(fine), np.sin(fine)
    turn = np.block([[cos, -sin], [sin, cos]])
    twist = 2.0 * math.pi * np.outer(q, r) / PADDED
    twist = np.repeat(twist, LANE_CH, 0)

    def half(a):
        return jnp.asarray(a, jnp.float32).astype(jnp.bfloat16)

    return (
        half(gather),
        half(spread),
        half(turn),
        jnp.asarray(np.cos(twist), jnp.float32),
        jnp.asarray(np.sin(twist), jnp.float32),
    )


def dot(a, b, contract=((1,), (0,))):
    return lax.dot_general(a, b, (contract, ((), ())), preferred_element_type=jnp.float32)


def bf16(a):
    return a.astype(jnp.bfloat16)


def turned(real, imag, cos, sin):
    c, s = cos[...], sin[...]
    return bf16(real * c + imag * s), bf16(imag * c - real * s)


def forward(a, tables):
    count = SLOTS * LANE_CH
    b = turned(a[:count], a[count:], tables["cos"], tables["sin"])
    spec = dot(jnp.concatenate(b, 1), tables["turn"][...])
    return spec[:, :ROWS], spec[:, ROWS:]


def inverse(real, imag, tables):
    y = jnp.concatenate([bf16(real), bf16(imag)], 1)
    z = dot(y, tables["turn"][...], ((1,), (1,)))
    imag, real = turned(z[:, ROWS:], z[:, :ROWS], tables["cos"], tables["sin"])
    return dot(tables["spread"][...], jnp.concatenate([real, imag], 0))


TABLES = ("gather", "cos", "sin", "turn", "spread")


class Fetch:
    def __init__(self, far, near, sems):
        self.near = dict(zip(TABLES, near))
        self.copies = {
            n: pltpu.make_async_copy(f, t, sems.at[i]) for i, (n, f, t) in enumerate(zip(TABLES, far, near))
        }

    def start(self, *names):
        for name in names:
            self.copies[name].start()

    def wait(self, *names):
        for name in names:
            self.copies[name].wait()


def chunks(a):
    return bf16(a).reshape(SEQ_PARTS, LANE_CH, ROWS)


def flat(a):
    return a.reshape(WIDTH, ROWS)


def prepare_kernel(inner, values, taps, skip, out):
    product = inner[...].astype(jnp.float32) * values[...].astype(jnp.float32)
    out[:, :LANE_CH, :] = chunks(product.T)
    first = lax.broadcasted_iota(jnp.int32, (ROWS, WIDTH), 0) == 0
    out[:, LANE_CH:, :] = chunks((taps[...] + jnp.where(first, skip[...], 0.0)).T)


def project_kernel(where, weight, grad, *refs):
    out, blocks, sems = refs[-3:]

    def copy(i):
        return pltpu.make_async_copy(weight.at[2 * i + where[1]], blocks.at[i], sems.at[i])

    @pl.loop(0, AHEAD)
    def _(i):
        copy(i).start()

    if len(refs) == 4:
        far_grad, grad = grad, refs[0]
        load = pltpu.make_async_copy(far_grad, grad, sems.at[4])
        load.start()
        load.wait()

    @pl.loop(0, 4)
    def _(i):
        copy(i).wait()

        @pl.when(i + AHEAD < 4)
        def _():
            copy(i + AHEAD).start()

        out[(i - where[0]) & 3] = bf16(dot(blocks[i], grad[...], ((1,), (1,))))


def add_kernel(where, kept, other, *outs):
    ahead = 1 + 2 * where[1]
    for slot, out in zip((2, 4 - ahead, ahead, 0), outs):
        out[...] = bf16(kept[slot].astype(jnp.float32) + other[slot].astype(jnp.float32))


def add_two_kernel(a, b, out):
    out[...] = bf16(a[...].astype(jnp.float32) + b[...].astype(jnp.float32))


def turn_kernel(outer, after, out):
    out[...] = bf16(outer[...].astype(jnp.float32).T)


def first_kernel(go, got, *refs):
    (conv, sr, si, tr, ti), kept, (sems, first) = refs[5:10], refs[10:15], refs[15:]
    fetch = Fetch(refs[:5], kept, sems)

    @pl.when(go[0] >= 0)
    def _():
        fetch.start("gather")
        fetch.wait("gather")
        fetch.start("cos", "sin", "turn", "spread")

    @pl.when(go[0] >= 0)
    def _():
        first[0] = dot(fetch.near["gather"][...], flat(got[:, :LANE_CH, :]))
        first[1] = dot(fetch.near["gather"][...], flat(got[:, LANE_CH:, :]))
        fetch.wait("cos", "sin", "turn")

    @pl.when(go[0] >= 0)
    def _():
        sr[...], si[...] = forward(first[0], fetch.near)
        tr[...], ti[...] = forward(first[1], fetch.near)
        fetch.wait("spread")

    x_real, x_imag, t_real, t_imag = sr[...], si[...], tr[...], ti[...]
    y = inverse(x_real * t_real - x_imag * t_imag, x_real * t_imag + x_imag * t_real, fetch.near)
    conv[...] = chunks(y)


def middle_kernel(own, a, b, outer_t, conv, out, hidden_grad_t):
    total = own[...].astype(jnp.float32) + (a[...].astype(jnp.float32) + b[...].astype(jnp.float32))
    hidden_grad_t[...] = total
    out[:, :LANE_CH, :] = chunks(total * outer_t[...].astype(jnp.float32))
    out[:, LANE_CH:, :] = conv[...]


def second_kernel(got, sr, si, tr, ti, *refs):
    tables, out = dict(zip(TABLES, refs)), refs[5]
    g_real, g_imag = forward(dot(tables["gather"][...], flat(got[:, :LANE_CH, :])), tables)
    t_real, t_imag = tr[...], ti[...]
    corr = inverse(t_real * g_real + t_imag * g_imag, t_real * g_imag - t_imag * g_real, tables)
    out[:, :LANE_CH, :] = chunks(corr)
    x_real, x_imag = sr[...], si[...]
    lag = inverse(x_real * g_real + x_imag * g_imag, x_real * g_imag - x_imag * g_real, tables)
    out[:, LANE_CH:, :] = chunks(lag)


def gate_kernel(got, outer, hidden_grad_t, hidden, outer_grad):
    mixed_pre = flat(got[:, LANE_CH:, :]).astype(jnp.float32)
    hidden[...] = bf16(outer[...].astype(jnp.float32) * mixed_pre.T)
    outer_grad[...] = bf16((hidden_grad_t[...] * mixed_pre).T)


def final_kernel(got, inner, values, inner_grad, values_grad, taps_grad):
    total = flat(got[:, :LANE_CH, :]).astype(jnp.float32).T
    inner_grad[...] = bf16(total * values[...].astype(jnp.float32))
    values_grad[...] = bf16(total * inner[...].astype(jnp.float32))
    taps_grad[...] = flat(got[:, LANE_CH:, :]).astype(jnp.float32).T


def fetch_kernel(weight, hidden, sent, out, sems):
    @pl.loop(0, 8)
    def _(i):
        pltpu.make_async_copy(weight.at[i], out.at[i], sems.at[i]).start()

    @pl.loop(0, 8)
    def _(i):
        pltpu.make_async_copy(weight.at[i], out.at[i], sems.at[i]).wait()


def mixed_kernel(where, *refs):
    parts, weight = refs[:4], refs[4]
    base = refs[5] if len(refs) == 7 else None
    out = refs[-1]
    for c in range(0, COLUMNS, 256):
        columns = slice(c, c + 256)
        total = None if base is None else base[:, columns]
        for i, part in enumerate(parts):
            slot = 2 * ((where[0] - i) & 3) + where[1]
            term = dot(part[...], weight[slot, :, columns])
            total = term if total is None else total + term
        out[:, columns] = total.astype(out.dtype)


def shape(dims, dtype):
    return jax.ShapeDtypeStruct(dims, dtype)


def inside(dims, dtype):
    return pltpu.VMEM(dims, dtype)


def outside(dims, dtype):
    return pltpu.HBM(dims, dtype)


VMEM = pl.BlockSpec(memory_space=pltpu.VMEM)
HBM = pl.BlockSpec(memory_space=pltpu.HBM)
SMEM = pl.BlockSpec(memory_space=pltpu.SMEM)


def local(kernel, outs, *args, limit=16, specs=None, scratch=(), hold=(), cost=0.0):
    n = len(args)

    def body(*refs):
        kernel(*refs[:n], *refs[n + len(hold) :])

    return pl.pallas_call(
        body,
        out_shape=outs,
        in_specs=list(specs or [VMEM] * n) + [VMEM] * len(hold),
        out_specs=tuple(VMEM for _ in outs),
        scratch_shapes=scratch,
        compiler_params=pltpu.CompilerParams(vmem_limit_bytes=limit << 20),
        cost_estimate=pl.CostEstimate(flops=int(cost * 1.15e9), bytes_accessed=1 << 16, transcendentals=0),
    )(*args, *map(near_memory, hold))


def far_memory(a):
    return pltpu.with_memory_space_constraint(a, pltpu.HBM)


def near_memory(a):
    return pltpu.with_memory_space_constraint(a, pltpu.VMEM)


def project(where, weight, grad, cost, load):
    out = inside((4, WIDTH, ROWS), jnp.bfloat16)
    return local(
        project_kernel,
        (inside(grad.shape, grad.dtype), out) if load else (out,),
        where,
        weight,
        far_memory(grad) if load else near_memory(grad),
        specs=[SMEM, HBM, HBM if load else VMEM],
        scratch=[pltpu.VMEM((4, WIDTH, COLUMNS), jnp.bfloat16), pltpu.SemaphoreType.DMA((5,))],
        cost=cost,
    )


def mix(where, parts, weight, extra, out):
    return local(
        mixed_kernel,
        (out((ROWS, COLUMNS), jnp.float32 if out is inside else jnp.bfloat16),),
        where,
        *parts,
        weight,
        *extra,
        specs=[SMEM] + [VMEM] * (5 + len(extra)),
        cost=COSTS[3] if out is inside else COSTS[4],
    )[0]


def exchange(a):
    return lax.all_to_all(a, "seq", split_axis=0, concat_axis=0, tiled=True)


def to_partner(a):
    return lax.ppermute(a, "ch", [(i, i ^ 1) for i in range(8)])


def along(a, way):
    pairs = [(2 * y + c, 2 * ((y + way * (1 - 2 * c)) % 4) + c) for y in range(4) for c in range(2)]
    return lax.ppermute(a, "ch", pairs)


def shifted(a, rows):
    return lax.ppermute(a, "ch", [(i, (i + 2 * rows) % 8) for i in range(8)])


def on_device(outer_gate, inner_gate, values, filter_taps, skip_scale, out_weight, out_grad):
    tables = [far_memory(transform_tables()[i]) for i in (0, 3, 4, 2, 1)]
    me = lax.axis_index("ch").astype(jnp.int32)
    row, core = me // 2, me % 2
    near_half, far_half = jnp.stack([row, core]), jnp.stack([row, 1 - core])
    block = (WIDTH, ROWS)
    block_row = (ROWS, WIDTH)
    sending = (SEQ_PARTS, 2 * LANE_CH, ROWS)
    weight = far_memory(out_weight.reshape(8, WIDTH, COLUMNS))

    skip = jnp.where(lax.axis_index("seq") == 0, skip_scale, 0.0).reshape(1, WIDTH)
    sent = local(
        prepare_kernel,
        (inside(sending, jnp.bfloat16),),
        *map(far_memory, (inner_gate, values, filter_taps)),
        skip,
        limit=8,
    )[0]
    sent, far_half, near_half = lax.optimization_barrier((sent, far_half, near_half))
    got = near_memory(exchange(sent))
    grad, given = project(far_half, weight, out_grad, COSTS[0], True)
    given, near_half = lax.optimization_barrier((given, near_half))
    kept = project(near_half, weight, grad, COSTS[1], False)[0]
    across, back, ahead, own = local(
        add_kernel,
        (inside(block, jnp.bfloat16),) * 3 + (outside(block, jnp.bfloat16),),
        near_half,
        kept,
        to_partner(given),
        specs=[SMEM, VMEM, VMEM],
    )
    passed = along(across, 1)
    back = along(back, -1)

    spectrum = inside((SLOTS * LANE_CH, ROWS), jnp.float32)
    conv, *kept = local(
        first_kernel,
        (
            inside((SEQ_PARTS, LANE_CH, ROWS), jnp.bfloat16),
            *(spectrum,) * 4,
            *(inside(t.shape, t.dtype) for t in tables),
        ),
        near_half,
        got,
        *tables,
        specs=[SMEM, VMEM] + [HBM] * len(tables),
        scratch=[
            pltpu.SemaphoreType.DMA((len(tables),)),
            pltpu.VMEM((2, 2 * SLOTS * LANE_CH, ROWS), jnp.float32),
        ],
        cost=COSTS[6],
    )
    ahead, conv = lax.optimization_barrier((ahead, conv))
    ahead = local(add_two_kernel, (inside(block, jnp.bfloat16),), ahead, passed)[0]
    outer_t = local(
        turn_kernel,
        (inside(block, jnp.bfloat16),),
        far_memory(outer_gate),
        ahead,
        cost=COSTS[5],
    )[0]
    sums = [far_memory(own), back, along(ahead, 1)]
    sent, hidden_grad_t = local(
        middle_kernel,
        (inside(sending, jnp.bfloat16), inside(block, jnp.float32)),
        *sums,
        outer_t,
        conv,
        hold=kept,
    )
    got = near_memory(exchange(sent))
    hidden, outer_grad = local(
        gate_kernel,
        (inside(block_row, jnp.bfloat16), outside(block_row, jnp.bfloat16)),
        got,
        far_memory(outer_gate),
        near_memory(hidden_grad_t),
        hold=kept,
    )
    sent = local(
        second_kernel,
        (outside(sending, jnp.bfloat16),),
        got,
        *map(near_memory, kept),
        hold=(hidden,),
    )[0]
    returned = near_memory(exchange(sent))
    near = [hidden, shifted(hidden, 1), shifted(hidden, 2), shifted(hidden, 3)]
    kept_weight = local(
        fetch_kernel,
        (inside(weight.shape, weight.dtype),),
        weight,
        hidden,
        far_memory(sent),
        specs=[HBM, VMEM, HBM],
        scratch=[pltpu.SemaphoreType.DMA((8,))],
        cost=COSTS[2],
    )[0]
    *waited, kept_weight = lax.optimization_barrier((*near, kept_weight))
    far = [to_partner(a) for a in waited]
    part = mix(near_half, near, kept_weight, (), inside)
    mixed = mix(far_half, far, kept_weight, (part,), outside)
    inner_grad, values_grad, taps_grad = local(
        final_kernel,
        (
            outside(block_row, jnp.bfloat16),
            outside(block_row, jnp.bfloat16),
            outside(block_row, jnp.float32),
        ),
        returned,
        inner_gate,
        values,
    )
    return (mixed, outer_grad, inner_grad, values_grad, taps_grad)


def solution(mesh):
    placed = (
        P("seq", "ch"),
        P("seq", "ch"),
        P("seq", "ch"),
        P("seq", "ch"),
        P("ch"),
        P(None, "ch"),
        P("seq", "ch"),
    )
    return jax.shard_map(
        on_device,
        mesh=mesh,
        in_specs=placed,
        out_specs=(P("seq", "ch"), P("seq", "ch"), P("seq", "ch"), P("seq", "ch"), P("seq", "ch")),
        check_vma=False,
    )
```

```python
import math

import jax
import jax.numpy as jnp
import numpy as np
from jax import lax
from jax.experimental import pallas as pl
from jax.experimental.pallas import tpu as pltpu
from jax.sharding import PartitionSpec as P

SEQ_PARTS = 32
ROWS = 256
WIDTH = 512
LANE_CH = WIDTH // SEQ_PARTS
COLUMNS = 1024
SLOTS = 32
PADDED = 2 * SEQ_PARTS * ROWS
AHEAD = 3
GROUP = 8
LINES = SLOTS * GROUP
LATE = False
COSTS = (0.0, 10.0, 2.0, 5.0, 0.0, 0.0, 0.0, 0.0, 20.0)


def transform_tables():
    q = np.arange(SLOTS) + 0.5
    p = np.arange(SEQ_PARTS)
    r = np.arange(ROWS)
    coarse = 2.0 * math.pi * np.outer(q, p) / (2 * SEQ_PARTS)
    eye = np.eye(GROUP)
    gather = np.concatenate([np.kron(np.cos(coarse), eye), np.kron(-np.sin(coarse), eye)], 0)
    spread = gather.T * (2.0 / PADDED)
    fine = 2.0 * math.pi * (np.outer(r, r) % ROWS) / ROWS
    cos, sin = np.cos(fine), np.sin(fine)
    turn = np.block([[cos, -sin], [sin, cos]])
    twist = 2.0 * math.pi * np.outer(q, r) / PADDED
    twist = np.repeat(twist, GROUP, 0)

    def half(a):
        return jnp.asarray(a, jnp.float32).astype(jnp.bfloat16)

    return (
        half(gather),
        half(spread),
        half(turn),
        jnp.asarray(np.cos(twist), jnp.float32),
        jnp.asarray(np.sin(twist), jnp.float32),
    )


def dot(a, b, contract=((1,), (0,))):
    return lax.dot_general(a, b, (contract, ((), ())), preferred_element_type=jnp.float32)


def bf16(a):
    return a.astype(jnp.bfloat16)


def turned(real, imag, cos, sin):
    c, s = cos[...], sin[...]
    return bf16(real * c + imag * s), bf16(imag * c - real * s)


def forward(x, tables):
    c, s = tables["cos"], tables["sin"]
    x = x.astype(jnp.float32)
    b = []
    for g in range(0, LANE_CH, GROUP):
        a = dot(tables["gather"][...], bf16(x[:, g : g + GROUP].reshape(SEQ_PARTS * GROUP, ROWS)))
        b.append(jnp.concatenate(turned(a[:LINES], a[LINES:], c, s), 1))
    spec = dot(jnp.concatenate(b, 0), tables["turn"][...])
    return spec[:, :ROWS], spec[:, ROWS:]


def inverse(real, imag, tables):
    c, s = tables["cos"], tables["sin"]
    y = jnp.concatenate([bf16(real), bf16(imag)], 1)
    z = dot(y, tables["turn"][...], ((1,), (1,)))
    out = []
    for g in range(0, 2 * LINES, LINES):
        imag, real = turned(z[g : g + LINES, ROWS:], z[g : g + LINES, :ROWS], c, s)
        y = dot(tables["spread"][...], jnp.concatenate([real, imag], 0))
        out.append(y.reshape(SEQ_PARTS, GROUP, ROWS))
    return bf16(jnp.concatenate(out, 1))


TABLES = ("gather", "cos", "sin", "turn", "spread")


class Fetch:
    def __init__(self, far, near, sems):
        self.near = dict(zip(TABLES, near))
        self.copies = {
            n: pltpu.make_async_copy(f, t, sems.at[i]) for i, (n, f, t) in enumerate(zip(TABLES, far, near))
        }

    def start(self, *names):
        for name in names:
            self.copies[name].start()

    def wait(self, *names):
        for name in names:
            self.copies[name].wait()


def chunks(a):
    return bf16(a).reshape(SEQ_PARTS, LANE_CH, ROWS)


def flat(a):
    return a.reshape(WIDTH, ROWS)


def prepare_kernel(inner, values, taps, skip, out):
    product = inner[...].astype(jnp.float32) * values[...].astype(jnp.float32)
    out[:, :LANE_CH, :] = chunks(product.T)
    first = lax.broadcasted_iota(jnp.int32, (ROWS, WIDTH), 0) == 0
    out[:, LANE_CH:, :] = chunks((taps[...] + jnp.where(first, skip[...], 0.0)).T)


def project_kernel(where, weight, grad, out, blocks, sems):

    def copy(i):
        return pltpu.make_async_copy(weight.at[2 * i + where[1]], blocks.at[i], sems.at[i])

    @pl.loop(0, AHEAD)
    def _(i):
        copy(i).start()

    @pl.loop(0, 4)
    def _(i):
        copy(i).wait()

        @pl.when(i + AHEAD < 4)
        def _():
            copy(i + AHEAD).start()

        out[(i - where[0]) & 3] = bf16(dot(blocks[i], grad[...], ((1,), (1,))))


def add_kernel(where, kept, other, *outs):
    ahead = 1 + 2 * where[1]
    for slot, out in zip((2, 4 - ahead, ahead, 0), outs):
        out[...] = bf16(kept[slot].astype(jnp.float32) + other[slot].astype(jnp.float32))


def add_two_kernel(ahead, passed, own, back, out, total):
    out[...] = bf16(ahead[...].astype(jnp.float32) + passed[...].astype(jnp.float32))
    total[...] = own[...].astype(jnp.float32) + back[...].astype(jnp.float32)


def turn_kernel(outer, after, out):
    out[...] = bf16(outer[...].astype(jnp.float32).T)


def first_kernel(go, got, *refs):
    (sr, si, tr, ti), kept, sems = refs[5:9], refs[9:14], refs[14]
    fetch = Fetch(refs[:5], kept, sems)

    @pl.when(go[0] >= 0)
    def _():
        fetch.start(*TABLES)
        fetch.wait("gather", "cos", "sin", "turn")

    @pl.when(go[0] >= 0)
    def _():
        sr[...], si[...] = forward(got[:, :LANE_CH, :], fetch.near)
        tr[...], ti[...] = forward(got[:, LANE_CH:, :], fetch.near)
        fetch.wait("spread")


def conv_kernel(sr, si, tr, ti, *refs):
    tables, conv = dict(zip(TABLES, refs)), refs[-1]
    x_real, x_imag, t_real, t_imag = sr[...], si[...], tr[...], ti[...]
    conv[...] = inverse(x_real * t_real - x_imag * t_imag, x_real * t_imag + x_imag * t_real, tables)


def middle_kernel(own, last, outer_t, conv, out, hidden_grad_t):
    total = own[...] + last[...].astype(jnp.float32)
    hidden_grad_t[...] = total
    out[:, :LANE_CH, :] = chunks(total * outer_t[...].astype(jnp.float32))
    out[:, LANE_CH:, :] = conv[...]


def second_kernel(got, sr, si, tr, ti, *refs):
    tables, out = dict(zip(TABLES, refs)), refs[-1]
    g_real, g_imag = forward(got[:, :LANE_CH, :], tables)
    t_real, t_imag = tr[...], ti[...]
    out[:, :LANE_CH, :] = inverse(
        t_real * g_real + t_imag * g_imag, t_real * g_imag - t_imag * g_real, tables
    )
    x_real, x_imag = sr[...], si[...]
    out[:, LANE_CH:, :] = inverse(
        x_real * g_real + x_imag * g_imag, x_real * g_imag - x_imag * g_real, tables
    )


def gate_kernel(where, got, outer, hidden_grad_t, hidden, outer_grad, staged, sem):
    copy = pltpu.make_async_copy(staged, outer_grad, sem)
    mixed_pre = flat(got[:, LANE_CH:, :]).astype(jnp.float32)

    @pl.when(where[0] >= 0)
    def _():
        staged[...] = bf16((hidden_grad_t[...] * mixed_pre).T)
        copy.start()

    hidden[...] = bf16(outer[...].astype(jnp.float32) * mixed_pre.T)
    copy.wait()


def final_kernel(got, inner, values, inner_grad, values_grad, taps_grad):
    total = flat(got[:, :LANE_CH, :]).astype(jnp.float32).T
    inner_grad[...] = bf16(total * values[...].astype(jnp.float32))
    values_grad[...] = bf16(total * inner[...].astype(jnp.float32))
    taps_grad[...] = flat(got[:, LANE_CH:, :]).astype(jnp.float32).T


def token_kernel(sent, hidden, out):
    out[...] = hidden[:8, :128]


def fetch_kernel(weight, hidden, sent, out, sems):
    @pl.loop(0, 8)
    def _(i):
        pltpu.make_async_copy(weight.at[i], out.at[i], sems.at[i]).start()

    @pl.loop(0, 8)
    def _(i):
        pltpu.make_async_copy(weight.at[i], out.at[i], sems.at[i]).wait()


def mixed_kernel(where, weight, *refs):
    parts, base, out = refs[:-2], refs[-2], refs[-1]
    blocks = (0, 1 - 2 * where[1], 2 * where[1] - 1) if len(parts) == 6 else (2,)
    blocks = [2 * ((where[0] + b) & 3) + where[1] for b in blocks]
    mirror = (0, 2 * where[1] - 1, 1 - 2 * where[1]) if len(parts) == 6 else (2,)
    blocks += [2 * ((where[0] + b) & 3) + 1 - where[1] for b in mirror]
    for c in range(0, COLUMNS, 256):
        columns = slice(c, c + 256)
        total = base[:, columns] if len(parts) == 2 else None
        for part, block in zip(parts, blocks):
            term = dot(part[...], weight[block, :, columns])
            total = term if total is None else total + term
        out[:, columns] = total.astype(out.dtype)


def shape(dims, dtype):
    return jax.ShapeDtypeStruct(dims, dtype)


def inside(dims, dtype):
    return pltpu.VMEM(dims, dtype)


def outside(dims, dtype):
    return pltpu.HBM(dims, dtype)


VMEM = pl.BlockSpec(memory_space=pltpu.VMEM)
HBM = pl.BlockSpec(memory_space=pltpu.HBM)
SMEM = pl.BlockSpec(memory_space=pltpu.SMEM)


def local(kernel, outs, *args, limit=16, specs=None, out_specs=None, scratch=(), hold=(), cost=0.0):
    n = len(args)

    def body(*refs):
        kernel(*refs[:n], *refs[n + len(hold) :])

    return pl.pallas_call(
        body,
        out_shape=outs,
        in_specs=list(specs or [VMEM] * n) + [VMEM] * len(hold),
        out_specs=out_specs or tuple(VMEM for _ in outs),
        scratch_shapes=scratch,
        compiler_params=pltpu.CompilerParams(vmem_limit_bytes=limit << 20),
        cost_estimate=pl.CostEstimate(flops=int(cost * 1.15e9), bytes_accessed=1 << 16, transcendentals=0),
    )(*args, *map(near_memory, hold))


def far_memory(a):
    return pltpu.with_memory_space_constraint(a, pltpu.HBM)


def near_memory(a):
    return pltpu.with_memory_space_constraint(a, pltpu.VMEM)


def project(where, weight, grad, cost):
    return local(
        project_kernel,
        (inside((4, WIDTH, ROWS), jnp.bfloat16),),
        where,
        weight,
        grad,
        specs=[SMEM, HBM, VMEM],
        scratch=[pltpu.VMEM((4, WIDTH, COLUMNS), jnp.bfloat16), pltpu.SemaphoreType.DMA((4,))],
        cost=cost,
    )[0]


def mix(where, weight, parts, base, out):
    return local(
        mixed_kernel,
        (out((ROWS, COLUMNS), jnp.float32 if out is inside else jnp.bfloat16),),
        where,
        weight,
        *parts,
        base,
        specs=[SMEM] + [VMEM] * (2 + len(parts)),
        cost=COSTS[3] if out is inside else COSTS[4],
    )[0]


def exchange(a):
    return lax.all_to_all(a, "seq", split_axis=0, concat_axis=0, tiled=True)


def to_partner(a):
    return lax.ppermute(a, "ch", [(i, i ^ 1) for i in range(8)])


def along(a, way):
    pairs = [(2 * y + c, 2 * ((y + way * (1 - 2 * c)) % 4) + c) for y in range(4) for c in range(2)]
    return lax.ppermute(a, "ch", pairs)


def on_device(outer_gate, inner_gate, values, filter_taps, skip_scale, out_weight, out_grad):
    tables = [far_memory(transform_tables()[i]) for i in (0, 3, 4, 2, 1)]
    me = lax.axis_index("ch").astype(jnp.int32)
    row, core = me // 2, me % 2
    near_half, far_half = jnp.stack([row, core]), jnp.stack([row, 1 - core])
    block = (WIDTH, ROWS)
    block_row = (ROWS, WIDTH)
    sending = (SEQ_PARTS, 2 * LANE_CH, ROWS)
    weight = far_memory(out_weight.reshape(8, WIDTH, COLUMNS))

    skip = jnp.where(lax.axis_index("seq") == 0, skip_scale, 0.0).reshape(1, WIDTH)
    sent = local(
        prepare_kernel,
        (inside(sending, jnp.bfloat16),),
        *map(far_memory, (inner_gate, values, filter_taps)),
        skip,
        limit=8,
        cost=COSTS[8],
    )[0]
    sent, far_half, near_half = lax.optimization_barrier((sent, far_half, near_half))
    got = near_memory(exchange(sent))
    given = project(far_half, weight, out_grad, COSTS[0])
    given, near_half = lax.optimization_barrier((given, near_half))
    kept = project(near_half, weight, out_grad, COSTS[1])
    across, back, ahead, own = local(
        add_kernel,
        (inside(block, jnp.bfloat16),) * 3 + (outside(block, jnp.bfloat16),),
        near_half,
        kept,
        to_partner(given),
        specs=[SMEM, VMEM, VMEM],
    )
    passed = along(across, 1)
    back = along(back, -1)

    spectrum = inside((SLOTS * LANE_CH, ROWS), jnp.float32)
    kept = local(
        first_kernel,
        (*(spectrum,) * 4, *(inside(t.shape, t.dtype) for t in tables)),
        near_half,
        got,
        *tables,
        specs=[SMEM, VMEM] + [HBM] * len(tables),
        scratch=[pltpu.SemaphoreType.DMA((len(tables),))],
        cost=COSTS[6],
    )
    ahead, total = local(
        add_two_kernel,
        (inside(block, jnp.bfloat16), inside(block, jnp.float32)),
        ahead,
        passed,
        far_memory(own),
        back,
        hold=kept[:1],
    )
    conv = local(
        conv_kernel,
        (inside((SEQ_PARTS, LANE_CH, ROWS), jnp.bfloat16),),
        *map(near_memory, kept),
        hold=(ahead,),
        cost=COSTS[7],
    )[0]
    outer_t = local(
        turn_kernel,
        (inside(block, jnp.bfloat16),),
        far_memory(outer_gate),
        ahead,
        cost=COSTS[5],
    )[0]
    sums = [near_memory(total), along(ahead, 1)]
    sent, hidden_grad_t = local(
        middle_kernel,
        (inside(sending, jnp.bfloat16), inside(block, jnp.float32)),
        *sums,
        outer_t,
        conv,
        hold=kept,
    )
    got = near_memory(exchange(sent))
    hidden, outer_grad = local(
        gate_kernel,
        (inside(block_row, jnp.bfloat16), outside(block_row, jnp.bfloat16)),
        near_half,
        got,
        outer_gate,
        near_memory(hidden_grad_t),
        specs=[SMEM, VMEM, VMEM, VMEM],
        out_specs=(VMEM, HBM),
        scratch=[pltpu.VMEM(block_row, jnp.bfloat16), pltpu.SemaphoreType.DMA],
        hold=kept,
    )
    sent = local(
        second_kernel,
        (outside(sending, jnp.bfloat16),),
        got,
        *map(near_memory, kept),
        hold=(hidden,),
    )[0]
    returned = near_memory(exchange(sent))
    before = along(hidden, 1)
    if LATE:
        after = None
    else:
        after = along(hidden, -1)
    token = local(
        token_kernel,
        (inside((8, 128), jnp.bfloat16),),
        far_memory(sent),
        hidden,
        specs=[HBM, VMEM],
    )[0]
    passed, turned_back, token = lax.optimization_barrier((before, hidden, token))
    if LATE:
        after = along(turned_back, -1)
    kept_weight = local(
        fetch_kernel,
        (inside(weight.shape, weight.dtype),),
        weight,
        token,
        far_memory(sent),
        specs=[HBM, VMEM, HBM],
        scratch=[pltpu.SemaphoreType.DMA((8,))],
        cost=COSTS[2],
    )[0]
    across = along(passed, 1)
    near = [hidden, after, before]
    far = [to_partner(a) for a in near]
    part = mix(near_half, kept_weight, near + far, hidden, inside)
    mixed = mix(near_half, kept_weight, [across, to_partner(across)], part, outside)
    inner_grad, values_grad, taps_grad = local(
        final_kernel,
        (
            outside(block_row, jnp.bfloat16),
            outside(block_row, jnp.bfloat16),
            outside(block_row, jnp.float32),
        ),
        returned,
        inner_gate,
        values,
    )
    return (mixed, outer_grad, inner_grad, values_grad, taps_grad)


def solution(mesh):
    placed = (
        P("seq", "ch"),
        P("seq", "ch"),
        P("seq", "ch"),
        P("seq", "ch"),
        P("ch"),
        P(None, "ch"),
        P("seq", "ch"),
    )
    return jax.shard_map(
        on_device,
        mesh=mesh,
        in_specs=placed,
        out_specs=(P("seq", "ch"), P("seq", "ch"), P("seq", "ch"), P("seq", "ch"), P("seq", "ch")),
        check_vma=False,
    )
```

```python
import math

import jax
import jax.numpy as jnp
import numpy as np
from jax import lax
from jax.experimental import pallas as pl
from jax.experimental.pallas import tpu as pltpu
from jax.sharding import PartitionSpec as P

SEQ_PARTS = 32
ROWS = 256
WIDTH = 512
LANE_CH = WIDTH // SEQ_PARTS
COLUMNS = 1024
SLOTS = 32
PADDED = 2 * SEQ_PARTS * ROWS
AHEAD = 3
GROUP = 8
LINES = SLOTS * GROUP
LATE = False
COSTS = (0.0, 10.0, 2.0, 5.0, 0.0, 0.0, 0.0, 0.0, 20.0)


def transform_tables():
    q = np.arange(SLOTS) + 0.5
    p = np.arange(SEQ_PARTS)
    r = np.arange(ROWS)
    coarse = 2.0 * math.pi * np.outer(q, p) / (2 * SEQ_PARTS)
    eye = np.eye(GROUP)
    gather = np.concatenate([np.kron(np.cos(coarse), eye), np.kron(-np.sin(coarse), eye)], 0)
    spread = gather.T * (2.0 / PADDED)
    fine = 2.0 * math.pi * (np.outer(r, r) % ROWS) / ROWS
    cos, sin = np.cos(fine), np.sin(fine)
    turn = np.block([[cos, -sin], [sin, cos]])
    twist = 2.0 * math.pi * np.outer(q, r) / PADDED
    twist = np.repeat(twist, GROUP, 0)

    def half(a):
        return jnp.asarray(a, jnp.float32).astype(jnp.bfloat16)

    return (
        half(gather),
        half(spread),
        half(turn),
        jnp.asarray(np.cos(twist), jnp.float32),
        jnp.asarray(np.sin(twist), jnp.float32),
    )


def dot(a, b, contract=((1,), (0,))):
    return lax.dot_general(a, b, (contract, ((), ())), preferred_element_type=jnp.float32)


def bf16(a):
    return a.astype(jnp.bfloat16)


def turned(real, imag, cos, sin):
    c, s = cos[...], sin[...]
    return bf16(real * c + imag * s), bf16(imag * c - real * s)


def gathered(x, tables):
    x = x.astype(jnp.float32)
    parts = (x[:, g : g + GROUP].reshape(SEQ_PARTS * GROUP, ROWS) for g in range(0, LANE_CH, GROUP))
    return [dot(tables["gather"][...], bf16(part)) for part in parts]


def transformed(parts, tables):
    c, s = tables["cos"], tables["sin"]
    b = [jnp.concatenate(turned(a[:LINES], a[LINES:], c, s), 1) for a in parts]
    spec = dot(jnp.concatenate(b, 0), tables["turn"][...])
    return spec[:, :ROWS], spec[:, ROWS:]


def forward(x, tables):
    return transformed(gathered(x, tables), tables)


def inverse(real, imag, tables):
    c, s = tables["cos"], tables["sin"]
    y = jnp.concatenate([bf16(real), bf16(imag)], 1)
    z = dot(y, tables["turn"][...], ((1,), (1,)))
    out = []
    for g in range(0, 2 * LINES, LINES):
        imag, real = turned(z[g : g + LINES, ROWS:], z[g : g + LINES, :ROWS], c, s)
        y = dot(tables["spread"][...], jnp.concatenate([real, imag], 0))
        out.append(y.reshape(SEQ_PARTS, GROUP, ROWS))
    return bf16(jnp.concatenate(out, 1))


TABLES = ("gather", "cos", "sin", "turn", "spread")


class Fetch:
    def __init__(self, far, near, sems):
        self.near = dict(zip(TABLES, near))
        self.copies = {
            n: pltpu.make_async_copy(f, t, sems.at[i]) for i, (n, f, t) in enumerate(zip(TABLES, far, near))
        }

    def start(self, *names):
        for name in names:
            self.copies[name].start()

    def wait(self, *names):
        for name in names:
            self.copies[name].wait()


def chunks(a):
    return bf16(a).reshape(SEQ_PARTS, LANE_CH, ROWS)


def flat(a):
    return a.reshape(WIDTH, ROWS)


def prepare_kernel(inner, values, taps, skip, out):
    product = inner[...].astype(jnp.float32) * values[...].astype(jnp.float32)
    out[:, :LANE_CH, :] = chunks(product.T)
    first = lax.broadcasted_iota(jnp.int32, (ROWS, WIDTH), 0) == 0
    out[:, LANE_CH:, :] = chunks((taps[...] + jnp.where(first, skip[...], 0.0)).T)


def project_kernel(first, where, weight, grad, out, blocks, sems):
    n = out.shape[0]

    def copy(i):
        block = 2 * ((where[0] + first + i) & 3) + where[1]
        return pltpu.make_async_copy(weight.at[block], blocks.at[i], sems.at[i])

    @pl.loop(0, min(n, AHEAD))
    def _(i):
        copy(i).start()

    @pl.loop(0, n)
    def _(i):
        copy(i).wait()

        @pl.when(i + AHEAD < n)
        def _():
            copy(i + AHEAD).start()

        out[i] = bf16(dot(blocks[i], grad[...], ((1,), (1,))))


def add_kernel(first, kept, other, *outs):
    for i, out in enumerate(outs):
        out[...] = bf16(kept[i].astype(jnp.float32) + other[first + i].astype(jnp.float32))


def sum_kernel(own, passed, total):
    total[...] = own[...].astype(jnp.float32) + passed[...].astype(jnp.float32)


def first_kernel(go, got, *refs):
    (sr, si, tr, ti), kept, (sems, parts) = refs[5:9], refs[9:14], refs[14:]
    fetch = Fetch(refs[:5], kept, sems)

    @pl.when(go[0] >= 0)
    def _():
        fetch.start(*TABLES)
        fetch.wait("gather")

    @pl.when(go[0] >= 0)
    def _():
        halves = (got[:, :LANE_CH, :], got[:, LANE_CH:, :])
        for i, part in enumerate(p for half in halves for p in gathered(half, fetch.near)):
            parts[i] = part
        fetch.wait("cos", "sin", "turn")

    @pl.when(go[0] >= 0)
    def _():
        sr[...], si[...] = transformed([parts[0], parts[1]], fetch.near)
        tr[...], ti[...] = transformed([parts[2], parts[3]], fetch.near)
        fetch.wait("spread")


def conv_kernel(sr, si, tr, ti, *refs):
    tables, (outer, conv, outer_t) = dict(zip(TABLES, refs)), refs[-3:]
    outer_t[...] = bf16(outer[...].astype(jnp.float32).T)
    x_real, x_imag, t_real, t_imag = sr[...], si[...], tr[...], ti[...]
    conv[...] = inverse(x_real * t_real - x_imag * t_imag, x_real * t_imag + x_imag * t_real, tables)


def middle_kernel(own, a, b, outer_t, conv, out, hidden_grad_t):
    total = own[...] + (a[...].astype(jnp.float32) + b[...].astype(jnp.float32))
    hidden_grad_t[...] = total
    out[:, :LANE_CH, :] = chunks(total * outer_t[...].astype(jnp.float32))
    out[:, LANE_CH:, :] = conv[...]


def second_kernel(got, sr, si, tr, ti, *refs):
    tables, out = dict(zip(TABLES, refs)), refs[-1]
    g_real, g_imag = forward(got[:, :LANE_CH, :], tables)
    t_real, t_imag = tr[...], ti[...]
    out[:, :LANE_CH, :] = inverse(
        t_real * g_real + t_imag * g_imag, t_real * g_imag - t_imag * g_real, tables
    )
    x_real, x_imag = sr[...], si[...]
    out[:, LANE_CH:, :] = inverse(
        x_real * g_real + x_imag * g_imag, x_real * g_imag - x_imag * g_real, tables
    )


def gate_kernel(where, got, outer, hidden_grad_t, hidden, outer_grad, staged, sem):
    copy = pltpu.make_async_copy(staged, outer_grad, sem)
    mixed_pre = flat(got[:, LANE_CH:, :]).astype(jnp.float32)

    @pl.when(where[0] >= 0)
    def _():
        staged[...] = bf16((hidden_grad_t[...] * mixed_pre).T)
        copy.start()

    hidden[...] = bf16(outer[...].astype(jnp.float32) * mixed_pre.T)
    copy.wait()


def final_kernel(got, inner, values, inner_grad, values_grad, taps_grad):
    total = flat(got[:, :LANE_CH, :]).astype(jnp.float32).T
    inner_grad[...] = bf16(total * values[...].astype(jnp.float32))
    values_grad[...] = bf16(total * inner[...].astype(jnp.float32))
    taps_grad[...] = flat(got[:, LANE_CH:, :]).astype(jnp.float32).T


def token_kernel(sent, hidden, out):
    out[...] = hidden[:8, :128]


def fetch_kernel(weight, hidden, sent, out, sems):
    @pl.loop(0, 8)
    def _(i):
        pltpu.make_async_copy(weight.at[i], out.at[i], sems.at[i]).start()

    @pl.loop(0, 8)
    def _(i):
        pltpu.make_async_copy(weight.at[i], out.at[i], sems.at[i]).wait()


def mixed_kernel(where, weight, *refs):
    parts, base, out = refs[:-2], refs[-2], refs[-1]
    blocks = (0, 1 - 2 * where[1], 2 * where[1] - 1) if len(parts) == 6 else (2,)
    blocks = [2 * ((where[0] + b) & 3) + where[1] for b in blocks]
    mirror = (0, 2 * where[1] - 1, 1 - 2 * where[1]) if len(parts) == 6 else (2,)
    blocks += [2 * ((where[0] + b) & 3) + 1 - where[1] for b in mirror]
    for c in range(0, COLUMNS, 256):
        columns = slice(c, c + 256)
        total = base[:, columns] if len(parts) == 2 else None
        for part, block in zip(parts, blocks):
            term = dot(part[...], weight[block, :, columns])
            total = term if total is None else total + term
        out[:, columns] = total.astype(out.dtype)


def shape(dims, dtype):
    return jax.ShapeDtypeStruct(dims, dtype)


def inside(dims, dtype):
    return pltpu.VMEM(dims, dtype)


def outside(dims, dtype):
    return pltpu.HBM(dims, dtype)


VMEM = pl.BlockSpec(memory_space=pltpu.VMEM)
HBM = pl.BlockSpec(memory_space=pltpu.HBM)
SMEM = pl.BlockSpec(memory_space=pltpu.SMEM)


def local(kernel, outs, *args, limit=16, specs=None, out_specs=None, scratch=(), hold=(), cost=0.0):
    n = len(args)

    def body(*refs):
        kernel(*refs[:n], *refs[n + len(hold) :])

    return pl.pallas_call(
        body,
        out_shape=outs,
        in_specs=list(specs or [VMEM] * n) + [VMEM] * len(hold),
        out_specs=out_specs or tuple(VMEM for _ in outs),
        scratch_shapes=scratch,
        compiler_params=pltpu.CompilerParams(vmem_limit_bytes=limit << 20),
        cost_estimate=pl.CostEstimate(flops=int(cost * 1.15e9), bytes_accessed=1 << 16, transcendentals=0),
    )(*args, *map(near_memory, hold))


def far_memory(a):
    return pltpu.with_memory_space_constraint(a, pltpu.HBM)


def near_memory(a):
    return pltpu.with_memory_space_constraint(a, pltpu.VMEM)


def project(first, count, where, weight, grad, cost):
    return local(
        lambda *refs: project_kernel(first, *refs),
        (inside((count, WIDTH, ROWS), jnp.bfloat16),),
        where,
        weight,
        grad,
        specs=[SMEM, HBM, VMEM],
        scratch=[pltpu.VMEM((count, WIDTH, COLUMNS), jnp.bfloat16), pltpu.SemaphoreType.DMA((count,))],
        cost=cost,
    )[0]


def mix(where, weight, parts, base, out):
    return local(
        mixed_kernel,
        (out((ROWS, COLUMNS), jnp.float32 if out is inside else jnp.bfloat16),),
        where,
        weight,
        *parts,
        base,
        specs=[SMEM] + [VMEM] * (2 + len(parts)),
        cost=COSTS[3] if out is inside else COSTS[4],
    )[0]


def exchange(a):
    return lax.all_to_all(a, "seq", split_axis=0, concat_axis=0, tiled=True)


def to_partner(a):
    return lax.ppermute(a, "ch", [(i, i ^ 1) for i in range(8)])


def along(a, way):
    pairs = [(2 * y + c, 2 * ((y + way * (1 - 2 * c)) % 4) + c) for y in range(4) for c in range(2)]
    return lax.ppermute(a, "ch", pairs)


def shifted(a, rows):
    return lax.ppermute(a, "ch", [(i, (i + 2 * rows) % 8) for i in range(8)])


def on_device(outer_gate, inner_gate, values, filter_taps, skip_scale, out_weight, out_grad):
    tables = [far_memory(transform_tables()[i]) for i in (0, 3, 4, 2, 1)]
    me = lax.axis_index("ch").astype(jnp.int32)
    row, core = me // 2, me % 2
    near_half, far_half = jnp.stack([row, core]), jnp.stack([row, 1 - core])
    block = (WIDTH, ROWS)
    block_row = (ROWS, WIDTH)
    sending = (SEQ_PARTS, 2 * LANE_CH, ROWS)
    weight = far_memory(out_weight.reshape(8, WIDTH, COLUMNS))

    skip = jnp.where(lax.axis_index("seq") == 0, skip_scale, 0.0).reshape(1, WIDTH)
    sent = local(
        prepare_kernel,
        (inside(sending, jnp.bfloat16),),
        *map(far_memory, (inner_gate, values, filter_taps)),
        skip,
        limit=8,
        cost=COSTS[8],
    )[0]
    sent, far_half, near_half = lax.optimization_barrier((sent, far_half, near_half))
    got = near_memory(exchange(sent))
    given = project(2, 4, far_half, weight, out_grad, COSTS[0])
    given, near_half = lax.optimization_barrier((given, near_half))
    kept = project(2, 1, near_half, weight, out_grad, COSTS[1])
    other = near_memory(to_partner(given))
    across = local(
        lambda *refs: add_kernel(0, *refs), (inside(block, jnp.bfloat16),), kept, other
    )[0]
    across, near_half = lax.optimization_barrier((across, near_half))
    kept = project(3, 3, near_half, weight, out_grad, COSTS[1])
    back, own, ahead = local(
        lambda *refs: add_kernel(1, *refs),
        (inside(block, jnp.bfloat16), outside(block, jnp.bfloat16), inside(block, jnp.bfloat16)),
        kept,
        other,
    )
    total = local(
        sum_kernel,
        (inside(block, jnp.float32),),
        far_memory(own),
        shifted(across, 2),
        hold=(got,),
    )[0]
    sums = [near_memory(total), shifted(ahead, 1), shifted(back, 3)]

    spectrum = inside((SLOTS * LANE_CH, ROWS), jnp.float32)
    kept = local(
        first_kernel,
        (*(spectrum,) * 4, *(inside(t.shape, t.dtype) for t in tables)),
        near_half,
        got,
        *tables,
        specs=[SMEM, VMEM] + [HBM] * len(tables),
        scratch=[
            pltpu.SemaphoreType.DMA((len(tables),)),
            pltpu.VMEM((4, 2 * LINES, ROWS), jnp.float32),
        ],
        hold=(total,),
        cost=COSTS[6],
    )
    conv, outer_t = local(
        conv_kernel,
        (inside((SEQ_PARTS, LANE_CH, ROWS), jnp.bfloat16), inside(block, jnp.bfloat16)),
        *map(near_memory, kept),
        outer_gate,
        cost=COSTS[7],
    )
    sent, hidden_grad_t = local(
        middle_kernel,
        (inside(sending, jnp.bfloat16), inside(block, jnp.float32)),
        *sums,
        outer_t,
        conv,
        hold=kept,
    )
    got = near_memory(exchange(sent))
    hidden, outer_grad = local(
        gate_kernel,
        (inside(block_row, jnp.bfloat16), outside(block_row, jnp.bfloat16)),
        near_half,
        got,
        outer_gate,
        near_memory(hidden_grad_t),
        specs=[SMEM, VMEM, VMEM, VMEM],
        out_specs=(VMEM, HBM),
        scratch=[pltpu.VMEM(block_row, jnp.bfloat16), pltpu.SemaphoreType.DMA],
        hold=kept,
    )
    sent = local(
        second_kernel,
        (outside(sending, jnp.bfloat16),),
        got,
        *map(near_memory, kept),
        hold=(hidden,),
    )[0]
    returned = near_memory(exchange(sent))
    before = along(hidden, 1)
    if LATE:
        after = None
    else:
        after = along(hidden, -1)
    token = local(
        token_kernel,
        (inside((8, 128), jnp.bfloat16),),
        far_memory(sent),
        hidden,
        specs=[HBM, VMEM],
    )[0]
    passed, turned_back, token = lax.optimization_barrier((before, hidden, token))
    if LATE:
        after = along(turned_back, -1)
    kept_weight = local(
        fetch_kernel,
        (inside(weight.shape, weight.dtype),),
        weight,
        token,
        far_memory(sent),
        specs=[HBM, VMEM, HBM],
        scratch=[pltpu.SemaphoreType.DMA((8,))],
        cost=COSTS[2],
    )[0]
    across = along(passed, 1)
    near = [hidden, after, before]
    far = [to_partner(a) for a in near]
    part = mix(near_half, kept_weight, near + far, hidden, inside)
    mixed = mix(near_half, kept_weight, [across, to_partner(across)], part, outside)
    inner_grad, values_grad, taps_grad = local(
        final_kernel,
        (
            outside(block_row, jnp.bfloat16),
            outside(block_row, jnp.bfloat16),
            outside(block_row, jnp.float32),
        ),
        returned,
        inner_gate,
        values,
    )
    return (mixed, outer_grad, inner_grad, values_grad, taps_grad)


def solution(mesh):
    placed = (
        P("seq", "ch"),
        P("seq", "ch"),
        P("seq", "ch"),
        P("seq", "ch"),
        P("ch"),
        P(None, "ch"),
        P("seq", "ch"),
    )
    return jax.shard_map(
        on_device,
        mesh=mesh,
        in_specs=placed,
        out_specs=(P("seq", "ch"), P("seq", "ch"), P("seq", "ch"), P("seq", "ch"), P("seq", "ch")),
        check_vma=False,
    )
```

```python
import math

import jax
import jax.numpy as jnp
import numpy as np
from jax import lax
from jax.experimental import pallas as pl
from jax.experimental.pallas import tpu as pltpu
from jax.sharding import PartitionSpec as P

SEQ_PARTS = 32
ROWS = 256
WIDTH = 512
LANE_CH = WIDTH // SEQ_PARTS
COLUMNS = 1024
SLOTS = 32
PADDED = 2 * SEQ_PARTS * ROWS
AHEAD = 3
GROUP = 8
LINES = SLOTS * GROUP
LATE = False
COSTS = (0.0, 10.0, 2.0, 5.0, 0.0, 0.0, 0.0, 0.0, 20.0)


def transform_tables():
    q = np.arange(SLOTS) + 0.5
    p = np.arange(SEQ_PARTS)
    r = np.arange(ROWS)
    coarse = 2.0 * math.pi * np.outer(q, p) / (2 * SEQ_PARTS)
    eye = np.eye(GROUP)
    gather = np.concatenate([np.kron(np.cos(coarse), eye), np.kron(-np.sin(coarse), eye)], 0)
    spread = gather.T * (2.0 / PADDED)
    fine = 2.0 * math.pi * (np.outer(r, r) % ROWS) / ROWS
    cos, sin = np.cos(fine), np.sin(fine)
    turn = np.block([[cos, -sin], [sin, cos]])
    twist = 2.0 * math.pi * np.outer(q, r) / PADDED
    twist = np.repeat(twist, GROUP, 0)

    def half(a):
        return jnp.asarray(a, jnp.float32).astype(jnp.bfloat16)

    return (
        half(gather),
        half(spread),
        half(turn),
        jnp.asarray(np.cos(twist), jnp.float32),
        jnp.asarray(np.sin(twist), jnp.float32),
    )


def dot(a, b, contract=((1,), (0,))):
    return lax.dot_general(a, b, (contract, ((), ())), preferred_element_type=jnp.float32)


def bf16(a):
    return a.astype(jnp.bfloat16)


def turned(real, imag, cos, sin):
    c, s = cos[...], sin[...]
    return bf16(real * c + imag * s), bf16(imag * c - real * s)


def gathered(x, tables):
    x = x.astype(jnp.float32)
    parts = (x[:, g : g + GROUP].reshape(SEQ_PARTS * GROUP, ROWS) for g in range(0, LANE_CH, GROUP))
    return [dot(tables["gather"][...], bf16(part)) for part in parts]


def transformed(parts, tables):
    c, s = tables["cos"], tables["sin"]
    b = [jnp.concatenate(turned(a[:LINES], a[LINES:], c, s), 1) for a in parts]
    spec = dot(jnp.concatenate(b, 0), tables["turn"][...])
    return spec[:, :ROWS], spec[:, ROWS:]


def forward(x, tables):
    return transformed(gathered(x, tables), tables)


def inverse(real, imag, tables):
    c, s = tables["cos"], tables["sin"]
    y = jnp.concatenate([bf16(real), bf16(imag)], 1)
    z = dot(y, tables["turn"][...], ((1,), (1,)))
    out = []
    for g in range(0, 2 * LINES, LINES):
        imag, real = turned(z[g : g + LINES, ROWS:], z[g : g + LINES, :ROWS], c, s)
        y = dot(tables["spread"][...], jnp.concatenate([real, imag], 0))
        out.append(y.reshape(SEQ_PARTS, GROUP, ROWS))
    return bf16(jnp.concatenate(out, 1))


TABLES = ("gather", "cos", "sin", "turn", "spread")


class Fetch:
    def __init__(self, far, near, sems):
        self.near = dict(zip(TABLES, near))
        self.copies = {
            n: pltpu.make_async_copy(f, t, sems.at[i]) for i, (n, f, t) in enumerate(zip(TABLES, far, near))
        }

    def start(self, *names):
        for name in names:
            self.copies[name].start()

    def wait(self, *names):
        for name in names:
            self.copies[name].wait()


def chunks(a):
    return bf16(a).reshape(SEQ_PARTS, LANE_CH, ROWS)


def flat(a):
    return a.reshape(WIDTH, ROWS)


def prepare_kernel(inner, values, taps, skip, out):
    product = inner[...].astype(jnp.float32) * values[...].astype(jnp.float32)
    out[:, :LANE_CH, :] = chunks(product.T)
    first = lax.broadcasted_iota(jnp.int32, (ROWS, WIDTH), 0) == 0
    out[:, LANE_CH:, :] = chunks((taps[...] + jnp.where(first, skip[...], 0.0)).T)


def project_kernel(first, where, weight, grad, out, blocks, sems):
    n = out.shape[0]

    def copy(i):
        block = 2 * ((where[0] + first + i) & 3) + where[1]
        return pltpu.make_async_copy(weight.at[block], blocks.at[i], sems.at[i])

    @pl.loop(0, min(n, AHEAD))
    def _(i):
        copy(i).start()

    @pl.loop(0, n)
    def _(i):
        copy(i).wait()

        @pl.when(i + AHEAD < n)
        def _():
            copy(i + AHEAD).start()

        out[i] = bf16(dot(blocks[i], grad[...], ((1,), (1,))))


def add_kernel(first, kept, other, *outs):
    for i, out in enumerate(outs):
        out[...] = bf16(kept[i].astype(jnp.float32) + other[first + i].astype(jnp.float32))


def first_kernel(go, got, *refs):
    far, own, (sr, si, tr, ti) = refs[:5], refs[5], refs[6:10]
    kept, own_near, (sems, parts) = refs[10:15], refs[15], refs[16:]
    fetch = Fetch(far, kept, sems)
    fetch_own = pltpu.make_async_copy(own, own_near, sems.at[len(TABLES)])

    @pl.when(go[0] >= 0)
    def _():
        fetch.start(*TABLES)
        fetch_own.start()
        fetch.wait("gather")

    @pl.when(go[0] >= 0)
    def _():
        halves = (got[:, :LANE_CH, :], got[:, LANE_CH:, :])
        for i, part in enumerate(p for half in halves for p in gathered(half, fetch.near)):
            parts[i] = part
        fetch.wait("cos", "sin", "turn")

    @pl.when(go[0] >= 0)
    def _():
        sr[...], si[...] = transformed([parts[0], parts[1]], fetch.near)
        tr[...], ti[...] = transformed([parts[2], parts[3]], fetch.near)
        fetch.wait("spread")
        fetch_own.wait()


def conv_kernel(sr, si, tr, ti, *refs):
    tables, (outer, conv, outer_t) = dict(zip(TABLES, refs)), refs[-3:]
    outer_t[...] = bf16(outer[...].astype(jnp.float32).T)
    x_real, x_imag, t_real, t_imag = sr[...], si[...], tr[...], ti[...]
    conv[...] = inverse(x_real * t_real - x_imag * t_imag, x_real * t_imag + x_imag * t_real, tables)


def middle_kernel(own, a, b, c, outer_t, conv, out, hidden_grad_t):
    total = (own[...].astype(jnp.float32) + a[...].astype(jnp.float32)) + (
        b[...].astype(jnp.float32) + c[...].astype(jnp.float32)
    )
    hidden_grad_t[...] = total
    out[:, :LANE_CH, :] = chunks(total * outer_t[...].astype(jnp.float32))
    out[:, LANE_CH:, :] = conv[...]


def second_kernel(got, gated, sr, si, tr, ti, *refs):
    tables, (out, outer_grad) = dict(zip(TABLES, refs)), refs[-2:]
    outer_grad[...] = gated[...]
    g_real, g_imag = forward(got[:, :LANE_CH, :], tables)
    t_real, t_imag = tr[...], ti[...]
    out[:, :LANE_CH, :] = inverse(
        t_real * g_real + t_imag * g_imag, t_real * g_imag - t_imag * g_real, tables
    )
    x_real, x_imag = sr[...], si[...]
    out[:, LANE_CH:, :] = inverse(
        x_real * g_real + x_imag * g_imag, x_real * g_imag - x_imag * g_real, tables
    )


def gate_kernel(got, outer, hidden_grad_t, hidden, gated):
    mixed_pre = flat(got[:, LANE_CH:, :]).astype(jnp.float32)
    hidden[...] = bf16(outer[...].astype(jnp.float32) * mixed_pre.T)
    gated[...] = bf16((hidden_grad_t[...] * mixed_pre).T)


def final_kernel(got, inner, values, inner_grad, values_grad, taps_grad):
    total = flat(got[:, :LANE_CH, :]).astype(jnp.float32).T
    inner_grad[...] = bf16(total * values[...].astype(jnp.float32))
    values_grad[...] = bf16(total * inner[...].astype(jnp.float32))
    taps_grad[...] = flat(got[:, LANE_CH:, :]).astype(jnp.float32).T


def token_kernel(sent, hidden, out):
    out[...] = hidden[:8, :128]


def fetch_kernel(weight, hidden, sent, out, sems):
    @pl.loop(0, 8)
    def _(i):
        pltpu.make_async_copy(weight.at[i], out.at[i], sems.at[i]).start()

    @pl.loop(0, 8)
    def _(i):
        pltpu.make_async_copy(weight.at[i], out.at[i], sems.at[i]).wait()


def mixed_kernel(where, weight, *refs):
    parts, base, out = refs[:-2], refs[-2], refs[-1]
    blocks = (0, 1 - 2 * where[1], 2 * where[1] - 1) if len(parts) == 6 else (2,)
    blocks = [2 * ((where[0] + b) & 3) + where[1] for b in blocks]
    mirror = (0, 2 * where[1] - 1, 1 - 2 * where[1]) if len(parts) == 6 else (2,)
    blocks += [2 * ((where[0] + b) & 3) + 1 - where[1] for b in mirror]
    for c in range(0, COLUMNS, 256):
        columns = slice(c, c + 256)
        total = base[:, columns] if len(parts) == 2 else None
        for part, block in zip(parts, blocks):
            term = dot(part[...], weight[block, :, columns])
            total = term if total is None else total + term
        out[:, columns] = total.astype(out.dtype)


def shape(dims, dtype):
    return jax.ShapeDtypeStruct(dims, dtype)


def inside(dims, dtype):
    return pltpu.VMEM(dims, dtype)


def outside(dims, dtype):
    return pltpu.HBM(dims, dtype)


VMEM = pl.BlockSpec(memory_space=pltpu.VMEM)
HBM = pl.BlockSpec(memory_space=pltpu.HBM)
SMEM = pl.BlockSpec(memory_space=pltpu.SMEM)


def local(kernel, outs, *args, limit=16, specs=None, out_specs=None, scratch=(), hold=(), cost=0.0):
    n = len(args)

    def body(*refs):
        kernel(*refs[:n], *refs[n + len(hold) :])

    return pl.pallas_call(
        body,
        out_shape=outs,
        in_specs=list(specs or [VMEM] * n) + [VMEM] * len(hold),
        out_specs=out_specs or tuple(VMEM for _ in outs),
        scratch_shapes=scratch,
        compiler_params=pltpu.CompilerParams(vmem_limit_bytes=limit << 20),
        cost_estimate=pl.CostEstimate(flops=int(cost * 1.15e9), bytes_accessed=1 << 16, transcendentals=0),
    )(*args, *map(near_memory, hold))


def far_memory(a):
    return pltpu.with_memory_space_constraint(a, pltpu.HBM)


def near_memory(a):
    return pltpu.with_memory_space_constraint(a, pltpu.VMEM)


def project(first, count, where, weight, grad, cost):
    return local(
        lambda *refs: project_kernel(first, *refs),
        (inside((count, WIDTH, ROWS), jnp.bfloat16),),
        where,
        weight,
        grad,
        specs=[SMEM, HBM, VMEM],
        scratch=[pltpu.VMEM((count, WIDTH, COLUMNS), jnp.bfloat16), pltpu.SemaphoreType.DMA((count,))],
        cost=cost,
    )[0]


def mix(where, weight, parts, base, out):
    return local(
        mixed_kernel,
        (out((ROWS, COLUMNS), jnp.float32 if out is inside else jnp.bfloat16),),
        where,
        weight,
        *parts,
        base,
        specs=[SMEM] + [VMEM] * (2 + len(parts)),
        cost=COSTS[3] if out is inside else COSTS[4],
    )[0]


def exchange(a):
    return lax.all_to_all(a, "seq", split_axis=0, concat_axis=0, tiled=True)


def to_partner(a):
    return lax.ppermute(a, "ch", [(i, i ^ 1) for i in range(8)])


def along(a, way):
    pairs = [(2 * y + c, 2 * ((y + way * (1 - 2 * c)) % 4) + c) for y in range(4) for c in range(2)]
    return lax.ppermute(a, "ch", pairs)


def shifted(a, rows):
    return lax.ppermute(a, "ch", [(i, (i + 2 * rows) % 8) for i in range(8)])


def on_device(outer_gate, inner_gate, values, filter_taps, skip_scale, out_weight, out_grad):
    tables = [far_memory(transform_tables()[i]) for i in (0, 3, 4, 2, 1)]
    me = lax.axis_index("ch").astype(jnp.int32)
    row, core = me // 2, me % 2
    near_half, far_half = jnp.stack([row, core]), jnp.stack([row, 1 - core])
    block = (WIDTH, ROWS)
    block_row = (ROWS, WIDTH)
    sending = (SEQ_PARTS, 2 * LANE_CH, ROWS)
    weight = far_memory(out_weight.reshape(8, WIDTH, COLUMNS))

    skip = jnp.where(lax.axis_index("seq") == 0, skip_scale, 0.0).reshape(1, WIDTH)
    sent = local(
        prepare_kernel,
        (inside(sending, jnp.bfloat16),),
        *map(far_memory, (inner_gate, values, filter_taps)),
        skip,
        limit=8,
        cost=COSTS[8],
    )[0]
    sent, far_half, near_half = lax.optimization_barrier((sent, far_half, near_half))
    got = near_memory(exchange(sent))
    given = project(2, 4, far_half, weight, out_grad, COSTS[0])
    given, near_half = lax.optimization_barrier((given, near_half))
    kept = project(2, 1, near_half, weight, out_grad, COSTS[1])
    other = near_memory(to_partner(given))
    across = local(
        lambda *refs: add_kernel(0, *refs), (inside(block, jnp.bfloat16),), kept, other
    )[0]
    across, near_half = lax.optimization_barrier((across, near_half))
    kept = project(3, 3, near_half, weight, out_grad, COSTS[1])
    back, own, ahead = local(
        lambda *refs: add_kernel(1, *refs),
        (inside(block, jnp.bfloat16), outside(block, jnp.bfloat16), inside(block, jnp.bfloat16)),
        kept,
        other,
    )
    across = near_memory(shifted(across, 2))
    sums = [across, shifted(ahead, 1), shifted(back, 3)]

    spectrum = inside((SLOTS * LANE_CH, ROWS), jnp.float32)
    *kept, own = local(
        first_kernel,
        (
            *(spectrum,) * 4,
            *(inside(t.shape, t.dtype) for t in tables),
            inside(block, jnp.bfloat16),
        ),
        near_half,
        got,
        *tables,
        far_memory(own),
        specs=[SMEM, VMEM] + [HBM] * (len(tables) + 1),
        scratch=[
            pltpu.SemaphoreType.DMA((len(tables) + 1,)),
            pltpu.VMEM((4, 2 * LINES, ROWS), jnp.float32),
        ],
        hold=(across,),
        cost=COSTS[6],
    )
    conv, outer_t = local(
        conv_kernel,
        (inside((SEQ_PARTS, LANE_CH, ROWS), jnp.bfloat16), inside(block, jnp.bfloat16)),
        *map(near_memory, kept),
        outer_gate,
        cost=COSTS[7],
    )
    sent, hidden_grad_t = local(
        middle_kernel,
        (inside(sending, jnp.bfloat16), inside(block, jnp.float32)),
        near_memory(own),
        *sums,
        outer_t,
        conv,
        hold=kept,
    )
    got = near_memory(exchange(sent))
    hidden, gated = local(
        gate_kernel,
        (inside(block_row, jnp.bfloat16), inside(block_row, jnp.bfloat16)),
        got,
        outer_gate,
        near_memory(hidden_grad_t),
        hold=kept,
    )
    sent, outer_grad = local(
        second_kernel,
        (outside(sending, jnp.bfloat16), outside(block_row, jnp.bfloat16)),
        got,
        *map(near_memory, (gated, *kept)),
        hold=(hidden,),
    )
    returned = near_memory(exchange(sent))
    before = along(hidden, 1)
    if LATE:
        after = None
    else:
        after = along(hidden, -1)
    token = local(
        token_kernel,
        (inside((8, 128), jnp.bfloat16),),
        far_memory(sent),
        hidden,
        specs=[HBM, VMEM],
    )[0]
    passed, turned_back, token = lax.optimization_barrier((before, hidden, token))
    if LATE:
        after = along(turned_back, -1)
    kept_weight = local(
        fetch_kernel,
        (inside(weight.shape, weight.dtype),),
        weight,
        token,
        far_memory(sent),
        specs=[HBM, VMEM, HBM],
        scratch=[pltpu.SemaphoreType.DMA((8,))],
        cost=COSTS[2],
    )[0]
    across = along(passed, 1)
    near = [hidden, after, before]
    far = [to_partner(a) for a in near]
    part = mix(near_half, kept_weight, near + far, hidden, inside)
    mixed = mix(near_half, kept_weight, [across, to_partner(across)], part, outside)
    inner_grad, values_grad, taps_grad = local(
        final_kernel,
        (
            outside(block_row, jnp.bfloat16),
            outside(block_row, jnp.bfloat16),
            outside(block_row, jnp.float32),
        ),
        returned,
        inner_gate,
        values,
    )
    return (mixed, outer_grad, inner_grad, values_grad, taps_grad)


def solution(mesh):
    placed = (
        P("seq", "ch"),
        P("seq", "ch"),
        P("seq", "ch"),
        P("seq", "ch"),
        P("ch"),
        P(None, "ch"),
        P("seq", "ch"),
    )
    return jax.shard_map(
        on_device,
        mesh=mesh,
        in_specs=placed,
        out_specs=(P("seq", "ch"), P("seq", "ch"), P("seq", "ch"), P("seq", "ch"), P("seq", "ch")),
        check_vma=False,
    )
```

```python
import math

import jax
import jax.numpy as jnp
import numpy as np
from jax import lax
from jax.experimental import pallas as pl
from jax.experimental.pallas import tpu as pltpu
from jax.sharding import PartitionSpec as P

SEQ_PARTS = 32
ROWS = 256
WIDTH = 512
LANE_CH = WIDTH // SEQ_PARTS
COLUMNS = 1024
SLOTS = 32
PADDED = 2 * SEQ_PARTS * ROWS
AHEAD = 3
GROUP = 8
LINES = SLOTS * GROUP
LATE = False
COSTS = (0.0, 10.0, 2.0, 5.0, 0.0, 0.0, 0.0, 0.0, 20.0)


def transform_tables():
    q = np.arange(SLOTS) + 0.5
    p = np.arange(SEQ_PARTS)
    r = np.arange(ROWS)
    coarse = 2.0 * math.pi * np.outer(q, p) / (2 * SEQ_PARTS)
    eye = np.eye(GROUP)
    gather = np.concatenate([np.kron(np.cos(coarse), eye), np.kron(-np.sin(coarse), eye)], 0)
    spread = gather.T * (2.0 / PADDED)
    fine = 2.0 * math.pi * (np.outer(r, r) % ROWS) / ROWS
    cos, sin = np.cos(fine), np.sin(fine)
    turn = np.block([[cos, -sin], [sin, cos]])
    twist = 2.0 * math.pi * np.outer(q, r) / PADDED
    twist = np.repeat(twist, GROUP, 0)

    def half(a):
        return jnp.asarray(a, jnp.float32).astype(jnp.bfloat16)

    return (
        half(gather),
        half(spread),
        half(turn),
        jnp.asarray(np.cos(twist), jnp.float32),
        jnp.asarray(np.sin(twist), jnp.float32),
    )


def dot(a, b, contract=((1,), (0,))):
    return lax.dot_general(a, b, (contract, ((), ())), preferred_element_type=jnp.float32)


def bf16(a):
    return a.astype(jnp.bfloat16)


def turned(real, imag, cos, sin):
    c, s = cos[...], sin[...]
    return bf16(real * c + imag * s), bf16(imag * c - real * s)


def gathered(x, tables):
    x = x.astype(jnp.float32)
    parts = (x[:, g : g + GROUP].reshape(SEQ_PARTS * GROUP, ROWS) for g in range(0, LANE_CH, GROUP))
    return [dot(tables["gather"][...], bf16(part)) for part in parts]


def transformed(parts, tables):
    c, s = tables["cos"], tables["sin"]
    b = [jnp.concatenate(turned(a[:LINES], a[LINES:], c, s), 1) for a in parts]
    spec = dot(jnp.concatenate(b, 0), tables["turn"][...])
    return spec[:, :ROWS], spec[:, ROWS:]


def forward(x, tables):
    return transformed(gathered(x, tables), tables)


def inverse(real, imag, tables):
    c, s = tables["cos"], tables["sin"]
    y = jnp.concatenate([bf16(real), bf16(imag)], 1)
    z = dot(y, tables["turn"][...], ((1,), (1,)))
    out = []
    for g in range(0, 2 * LINES, LINES):
        imag, real = turned(z[g : g + LINES, ROWS:], z[g : g + LINES, :ROWS], c, s)
        y = dot(tables["spread"][...], jnp.concatenate([real, imag], 0))
        out.append(y.reshape(SEQ_PARTS, GROUP, ROWS))
    return bf16(jnp.concatenate(out, 1))


TABLES = ("gather", "cos", "sin", "turn", "spread")


class Fetch:
    def __init__(self, far, near, sems):
        self.near = dict(zip(TABLES, near))
        self.copies = {
            n: pltpu.make_async_copy(f, t, sems.at[i]) for i, (n, f, t) in enumerate(zip(TABLES, far, near))
        }

    def start(self, *names):
        for name in names:
            self.copies[name].start()

    def wait(self, *names):
        for name in names:
            self.copies[name].wait()


def chunks(a):
    return bf16(a).reshape(SEQ_PARTS, LANE_CH, ROWS)


def flat(a):
    return a.reshape(WIDTH, ROWS)


def prepare_kernel(inner, values, taps, skip, out):
    product = inner[...].astype(jnp.float32) * values[...].astype(jnp.float32)
    out[:, :LANE_CH, :] = chunks(product.T)
    first = lax.broadcasted_iota(jnp.int32, (ROWS, WIDTH), 0) == 0
    out[:, LANE_CH:, :] = chunks((taps[...] + jnp.where(first, skip[...], 0.0)).T)


def project_kernel(first, where, weight, grad, out, blocks, sems):
    n = out.shape[0]

    def copy(i):
        block = 2 * ((where[0] + first + i) & 3) + where[1]
        return pltpu.make_async_copy(weight.at[block], blocks.at[i], sems.at[i])

    @pl.loop(0, min(n, AHEAD))
    def _(i):
        copy(i).start()

    @pl.loop(0, n)
    def _(i):
        copy(i).wait()

        @pl.when(i + AHEAD < n)
        def _():
            copy(i + AHEAD).start()

        out[i] = bf16(dot(blocks[i], grad[...], ((1,), (1,))))


def add_kernel(first, kept, other, *outs):
    for i, out in enumerate(outs):
        out[...] = bf16(kept[i].astype(jnp.float32) + other[first + i].astype(jnp.float32))


def first_kernel(go, got, *refs):
    far, own, (sr, si, tr, ti) = refs[:5], refs[5], refs[6:10]
    kept, own_near, (sems, parts) = refs[10:15], refs[15], refs[16:]
    fetch = Fetch(far, kept, sems)
    fetch_own = pltpu.make_async_copy(own, own_near, sems.at[len(TABLES)])

    @pl.when(go[0] >= 0)
    def _():
        fetch.start(*TABLES)
        fetch_own.start()
        fetch.wait("gather")

    @pl.when(go[0] >= 0)
    def _():
        halves = (got[:, :LANE_CH, :], got[:, LANE_CH:, :])
        for i, part in enumerate(p for half in halves for p in gathered(half, fetch.near)):
            parts[i] = part
        fetch.wait("cos", "sin", "turn")

    @pl.when(go[0] >= 0)
    def _():
        sr[...], si[...] = transformed([parts[0], parts[1]], fetch.near)
        tr[...], ti[...] = transformed([parts[2], parts[3]], fetch.near)
        fetch.wait("spread")
        fetch_own.wait()


def conv_kernel(sr, si, tr, ti, *refs):
    tables, (outer, conv, outer_t) = dict(zip(TABLES, refs)), refs[-3:]
    outer_t[...] = bf16(outer[...].astype(jnp.float32).T)
    x_real, x_imag, t_real, t_imag = sr[...], si[...], tr[...], ti[...]
    conv[...] = inverse(x_real * t_real - x_imag * t_imag, x_real * t_imag + x_imag * t_real, tables)


def middle_kernel(own, a, b, c, outer_t, conv, out, hidden_grad_t):
    total = (own[...].astype(jnp.float32) + a[...].astype(jnp.float32)) + (
        b[...].astype(jnp.float32) + c[...].astype(jnp.float32)
    )
    hidden_grad_t[...] = total
    out[:, :LANE_CH, :] = chunks(total * outer_t[...].astype(jnp.float32))
    out[:, LANE_CH:, :] = conv[...]


def second_kernel(got, gated, sr, si, tr, ti, *refs):
    tables, (out, outer_grad) = dict(zip(TABLES, refs)), refs[-2:]
    outer_grad[...] = gated[...]
    g_real, g_imag = forward(got[:, :LANE_CH, :], tables)
    t_real, t_imag = tr[...], ti[...]
    out[:, :LANE_CH, :] = inverse(
        t_real * g_real + t_imag * g_imag, t_real * g_imag - t_imag * g_real, tables
    )
    x_real, x_imag = sr[...], si[...]
    out[:, LANE_CH:, :] = inverse(
        x_real * g_real + x_imag * g_imag, x_real * g_imag - x_imag * g_real, tables
    )


def gate_kernel(got, outer, hidden_grad_t, hidden, gated):
    mixed_pre = flat(got[:, LANE_CH:, :]).astype(jnp.float32)
    hidden[...] = bf16(outer[...].astype(jnp.float32) * mixed_pre.T)
    gated[...] = bf16((hidden_grad_t[...] * mixed_pre).T)


def final_kernel(got, inner, values, inner_grad, values_grad, taps_grad):
    total = flat(got[:, :LANE_CH, :]).astype(jnp.float32).T
    inner_grad[...] = bf16(total * values[...].astype(jnp.float32))
    values_grad[...] = bf16(total * inner[...].astype(jnp.float32))
    taps_grad[...] = flat(got[:, LANE_CH:, :]).astype(jnp.float32).T


def token_kernel(sent, hidden, out):
    out[...] = hidden[:16, :128]


def fetch_kernel(weight, hidden, sent, out, sems):
    @pl.loop(0, 8)
    def _(i):
        pltpu.make_async_copy(weight.at[i], out.at[i], sems.at[i]).start()

    @pl.loop(0, 8)
    def _(i):
        pltpu.make_async_copy(weight.at[i], out.at[i], sems.at[i]).wait()


def mixed_kernel(where, weight, *refs):
    parts, base, out = refs[:-2], refs[-2], refs[-1]
    blocks = (0, 1 - 2 * where[1], 2 * where[1] - 1) if len(parts) == 6 else (2,)
    blocks = [2 * ((where[0] + b) & 3) + where[1] for b in blocks]
    mirror = (0, 2 * where[1] - 1, 1 - 2 * where[1]) if len(parts) == 6 else (2,)
    blocks += [2 * ((where[0] + b) & 3) + 1 - where[1] for b in mirror]
    for c in range(0, COLUMNS, 256):
        columns = slice(c, c + 256)
        total = base[:, columns] if len(parts) == 2 else None
        for part, block in zip(parts, blocks):
            term = dot(part[...], weight[block, :, columns])
            total = term if total is None else total + term
        out[:, columns] = total.astype(out.dtype)


def shape(dims, dtype):
    return jax.ShapeDtypeStruct(dims, dtype)


def inside(dims, dtype):
    return pltpu.VMEM(dims, dtype)


def outside(dims, dtype):
    return pltpu.HBM(dims, dtype)


VMEM = pl.BlockSpec(memory_space=pltpu.VMEM)
HBM = pl.BlockSpec(memory_space=pltpu.HBM)
SMEM = pl.BlockSpec(memory_space=pltpu.SMEM)


def local(kernel, outs, *args, limit=16, specs=None, out_specs=None, scratch=(), hold=(), cost=0.0):
    n = len(args)

    def body(*refs):
        kernel(*refs[:n], *refs[n + len(hold) :])

    return pl.pallas_call(
        body,
        out_shape=outs,
        in_specs=list(specs or [VMEM] * n) + [VMEM] * len(hold),
        out_specs=out_specs or tuple(VMEM for _ in outs),
        scratch_shapes=scratch,
        compiler_params=pltpu.CompilerParams(vmem_limit_bytes=limit << 20),
        cost_estimate=pl.CostEstimate(flops=int(cost * 1.15e9), bytes_accessed=1 << 16, transcendentals=0),
    )(*args, *map(near_memory, hold))


def far_memory(a):
    return pltpu.with_memory_space_constraint(a, pltpu.HBM)


def near_memory(a):
    return pltpu.with_memory_space_constraint(a, pltpu.VMEM)


def project(first, count, where, weight, grad, cost):
    return local(
        lambda *refs: project_kernel(first, *refs),
        (inside((count, WIDTH, ROWS), jnp.bfloat16),),
        where,
        weight,
        grad,
        specs=[SMEM, HBM, VMEM],
        scratch=[pltpu.VMEM((count, WIDTH, COLUMNS), jnp.bfloat16), pltpu.SemaphoreType.DMA((count,))],
        cost=cost,
    )[0]


def mix(where, weight, parts, base, out):
    return local(
        mixed_kernel,
        (out((ROWS, COLUMNS), jnp.float32 if out is inside else jnp.bfloat16),),
        where,
        weight,
        *parts,
        base,
        specs=[SMEM] + [VMEM] * (2 + len(parts)),
        cost=COSTS[3] if out is inside else COSTS[4],
    )[0]


def exchange(a):
    return lax.all_to_all(a, "seq", split_axis=0, concat_axis=0, tiled=True)


def to_partner(a):
    return lax.ppermute(a, "ch", [(i, i ^ 1) for i in range(8)])


def along(a, way):
    pairs = [(2 * y + c, 2 * ((y + way * (1 - 2 * c)) % 4) + c) for y in range(4) for c in range(2)]
    return lax.ppermute(a, "ch", pairs)


def shifted(a, rows):
    return lax.ppermute(a, "ch", [(i, (i + 2 * rows) % 8) for i in range(8)])


def on_device(outer_gate, inner_gate, values, filter_taps, skip_scale, out_weight, out_grad):
    tables = [far_memory(transform_tables()[i]) for i in (0, 3, 4, 2, 1)]
    me = lax.axis_index("ch").astype(jnp.int32)
    row, core = me // 2, me % 2
    near_half, far_half = jnp.stack([row, core]), jnp.stack([row, 1 - core])
    block = (WIDTH, ROWS)
    block_row = (ROWS, WIDTH)
    sending = (SEQ_PARTS, 2 * LANE_CH, ROWS)
    weight = far_memory(out_weight.reshape(8, WIDTH, COLUMNS))

    skip = jnp.where(lax.axis_index("seq") == 0, skip_scale, 0.0).reshape(1, WIDTH)
    sent = local(
        prepare_kernel,
        (inside(sending, jnp.bfloat16),),
        *map(far_memory, (inner_gate, values, filter_taps)),
        skip,
        limit=8,
        cost=COSTS[8],
    )[0]
    sent, far_half, near_half = lax.optimization_barrier((sent, far_half, near_half))
    got = near_memory(exchange(sent))
    given = project(2, 4, far_half, weight, out_grad, COSTS[0])
    given, near_half = lax.optimization_barrier((given, near_half))
    kept = project(2, 1, near_half, weight, out_grad, COSTS[1])
    other = near_memory(to_partner(given))
    across = local(
        lambda *refs: add_kernel(0, *refs), (inside(block, jnp.bfloat16),), kept, other
    )[0]
    across, near_half = lax.optimization_barrier((across, near_half))
    kept = project(3, 3, near_half, weight, out_grad, COSTS[1])
    back, own, ahead = local(
        lambda *refs: add_kernel(1, *refs),
        (inside(block, jnp.bfloat16), outside(block, jnp.bfloat16), inside(block, jnp.bfloat16)),
        kept,
        other,
    )
    across = near_memory(shifted(across, 2))
    sums = [across, shifted(ahead, 1), shifted(back, 3)]

    spectrum = inside((SLOTS * LANE_CH, ROWS), jnp.float32)
    *kept, own = local(
        first_kernel,
        (
            *(spectrum,) * 4,
            *(inside(t.shape, t.dtype) for t in tables),
            inside(block, jnp.bfloat16),
        ),
        near_half,
        got,
        *tables,
        far_memory(own),
        specs=[SMEM, VMEM] + [HBM] * (len(tables) + 1),
        scratch=[
            pltpu.SemaphoreType.DMA((len(tables) + 1,)),
            pltpu.VMEM((4, 2 * LINES, ROWS), jnp.float32),
        ],
        hold=(across,),
        cost=COSTS[6],
    )
    conv, outer_t = local(
        conv_kernel,
        (inside((SEQ_PARTS, LANE_CH, ROWS), jnp.bfloat16), inside(block, jnp.bfloat16)),
        *map(near_memory, kept),
        outer_gate,
        cost=COSTS[7],
    )
    sent, hidden_grad_t = local(
        middle_kernel,
        (inside(sending, jnp.bfloat16), inside(block, jnp.float32)),
        near_memory(own),
        *sums,
        outer_t,
        conv,
        hold=kept,
    )
    got = near_memory(exchange(sent))
    hidden, gated = local(
        gate_kernel,
        (inside(block_row, jnp.bfloat16), inside(block_row, jnp.bfloat16)),
        got,
        outer_gate,
        near_memory(hidden_grad_t),
        hold=kept,
    )
    sent, outer_grad = local(
        second_kernel,
        (outside(sending, jnp.bfloat16), outside(block_row, jnp.bfloat16)),
        got,
        *map(near_memory, (gated, *kept)),
        hold=(hidden,),
    )
    returned = near_memory(exchange(sent))
    before = along(hidden, 1)
    if LATE:
        after = None
    else:
        after = along(hidden, -1)
    token = local(
        token_kernel,
        (inside((16, 128), jnp.bfloat16),),
        far_memory(sent),
        hidden,
        specs=[HBM, VMEM],
    )[0]
    passed, turned_back, token = lax.optimization_barrier((before, hidden, token))
    if LATE:
        after = along(turned_back, -1)
    kept_weight = local(
        fetch_kernel,
        (inside(weight.shape, weight.dtype),),
        weight,
        token,
        far_memory(sent),
        specs=[HBM, VMEM, HBM],
        scratch=[pltpu.SemaphoreType.DMA((8,))],
        cost=COSTS[2],
    )[0]
    across = along(passed, 1)
    near = [hidden, after, before]
    far = [to_partner(a) for a in near]
    part = mix(near_half, kept_weight, near + far, hidden, inside)
    mixed = mix(near_half, kept_weight, [across, to_partner(across)], part, outside)
    inner_grad, values_grad, taps_grad = local(
        final_kernel,
        (
            outside(block_row, jnp.bfloat16),
            outside(block_row, jnp.bfloat16),
            outside(block_row, jnp.float32),
        ),
        returned,
        inner_gate,
        values,
    )
    return (mixed, outer_grad, inner_grad, values_grad, taps_grad)


def solution(mesh):
    placed = (
        P("seq", "ch"),
        P("seq", "ch"),
        P("seq", "ch"),
        P("seq", "ch"),
        P("ch"),
        P(None, "ch"),
        P("seq", "ch"),
    )
    return jax.shard_map(
        on_device,
        mesh=mesh,
        in_specs=placed,
        out_specs=(P("seq", "ch"), P("seq", "ch"), P("seq", "ch"), P("seq", "ch"), P("seq", "ch")),
        check_vma=False,
    )
```

```python
import math

import jax
import jax.numpy as jnp
import numpy as np
from jax import lax
from jax.experimental import pallas as pl
from jax.experimental.pallas import tpu as pltpu
from jax.sharding import PartitionSpec as P

SEQ_PARTS = 32
ROWS = 256
WIDTH = 512
LANE_CH = WIDTH // SEQ_PARTS
COLUMNS = 1024
SLOTS = 32
PADDED = 2 * SEQ_PARTS * ROWS
AHEAD = 3
GROUP = 8
LINES = SLOTS * GROUP
LATE = False
COSTS = (0.0, 10.0, 2.0, 5.0, 0.0, 0.0, 0.0, 0.0, 20.0)


def transform_tables():
    q = np.arange(SLOTS) + 0.5
    p = np.arange(SEQ_PARTS)
    r = np.arange(ROWS)
    coarse = 2.0 * math.pi * np.outer(q, p) / (2 * SEQ_PARTS)
    eye = np.eye(GROUP)
    gather = np.concatenate([np.kron(np.cos(coarse), eye), np.kron(-np.sin(coarse), eye)], 0)
    spread = gather.T * (2.0 / PADDED)
    fine = 2.0 * math.pi * (np.outer(r, r) % ROWS) / ROWS
    cos, sin = np.cos(fine), np.sin(fine)
    turn = np.block([[cos, -sin], [sin, cos]])
    twist = 2.0 * math.pi * np.outer(q, r) / PADDED
    twist = np.repeat(twist, GROUP, 0)

    def half(a):
        return jnp.asarray(a, jnp.float32).astype(jnp.bfloat16)

    return (
        half(gather),
        half(spread),
        half(turn),
        jnp.asarray(np.cos(twist), jnp.float32),
        jnp.asarray(np.sin(twist), jnp.float32),
    )


def dot(a, b, contract=((1,), (0,))):
    return lax.dot_general(a, b, (contract, ((), ())), preferred_element_type=jnp.float32)


def bf16(a):
    return a.astype(jnp.bfloat16)


def turned(real, imag, cos, sin):
    c, s = cos[...], sin[...]
    return bf16(real * c + imag * s), bf16(imag * c - real * s)


def gathered(x, tables):
    x = x.astype(jnp.float32)
    parts = (x[:, g : g + GROUP].reshape(SEQ_PARTS * GROUP, ROWS) for g in range(0, LANE_CH, GROUP))
    return [dot(tables["gather"][...], bf16(part)) for part in parts]


def transformed(parts, tables):
    c, s = tables["cos"], tables["sin"]
    b = [jnp.concatenate(turned(a[:LINES], a[LINES:], c, s), 1) for a in parts]
    spec = dot(jnp.concatenate(b, 0), tables["turn"][...])
    return spec[:, :ROWS], spec[:, ROWS:]


def forward(x, tables):
    return transformed(gathered(x, tables), tables)


def inverse(real, imag, tables):
    c, s = tables["cos"], tables["sin"]
    y = jnp.concatenate([bf16(real), bf16(imag)], 1)
    z = dot(y, tables["turn"][...], ((1,), (1,)))
    out = []
    for g in range(0, 2 * LINES, LINES):
        imag, real = turned(z[g : g + LINES, ROWS:], z[g : g + LINES, :ROWS], c, s)
        y = dot(tables["spread"][...], jnp.concatenate([real, imag], 0))
        out.append(y.reshape(SEQ_PARTS, GROUP, ROWS))
    return bf16(jnp.concatenate(out, 1))


TABLES = ("gather", "cos", "sin", "turn", "spread")


class Fetch:
    def __init__(self, far, near, sems):
        self.near = dict(zip(TABLES, near))
        self.copies = {
            n: pltpu.make_async_copy(f, t, sems.at[i]) for i, (n, f, t) in enumerate(zip(TABLES, far, near))
        }

    def start(self, *names):
        for name in names:
            self.copies[name].start()

    def wait(self, *names):
        for name in names:
            self.copies[name].wait()


def chunks(a):
    return bf16(a).reshape(SEQ_PARTS, LANE_CH, ROWS)


def flat(a):
    return a.reshape(WIDTH, ROWS)


def prepare_kernel(inner, values, taps, skip, out):
    product = inner[...].astype(jnp.float32) * values[...].astype(jnp.float32)
    out[:, :LANE_CH, :] = chunks(product.T)
    first = lax.broadcasted_iota(jnp.int32, (ROWS, WIDTH), 0) == 0
    out[:, LANE_CH:, :] = chunks((taps[...] + jnp.where(first, skip[...], 0.0)).T)


def project_kernel(first, where, weight, grad, out, blocks, sems):
    n = out.shape[0]

    def copy(i):
        block = 2 * ((where[0] + first + i) & 3) + where[1]
        return pltpu.make_async_copy(weight.at[block], blocks.at[i], sems.at[i])

    @pl.loop(0, min(n, AHEAD))
    def _(i):
        copy(i).start()

    @pl.loop(0, n)
    def _(i):
        copy(i).wait()

        @pl.when(i + AHEAD < n)
        def _():
            copy(i + AHEAD).start()

        out[i] = bf16(dot(blocks[i], grad[...], ((1,), (1,))))


def add_kernel(first, kept, other, *outs):
    for i, out in enumerate(outs):
        out[...] = bf16(kept[i].astype(jnp.float32) + other[first + i].astype(jnp.float32))


def first_kernel(go, got, *refs):
    far, own, (sr, si, tr, ti) = refs[:5], refs[5], refs[6:10]
    kept, own_near, (sems, parts) = refs[10:15], refs[15], refs[16:]
    fetch = Fetch(far, kept, sems)
    fetch_own = pltpu.make_async_copy(own, own_near, sems.at[len(TABLES)])

    @pl.when(go[0] >= 0)
    def _():
        fetch.start(*TABLES)
        fetch_own.start()
        fetch.wait("gather")

    @pl.when(go[0] >= 0)
    def _():
        halves = (got[:, :LANE_CH, :], got[:, LANE_CH:, :])
        for i, part in enumerate(p for half in halves for p in gathered(half, fetch.near)):
            parts[i] = part
        fetch.wait("cos", "sin", "turn")

    @pl.when(go[0] >= 0)
    def _():
        sr[...], si[...] = transformed([parts[0], parts[1]], fetch.near)
        tr[...], ti[...] = transformed([parts[2], parts[3]], fetch.near)
        fetch.wait("spread")
        fetch_own.wait()


def conv_kernel(sr, si, tr, ti, *refs):
    tables, (outer, conv, outer_t) = dict(zip(TABLES, refs)), refs[-3:]
    outer_t[...] = bf16(outer[...].astype(jnp.float32).T)
    x_real, x_imag, t_real, t_imag = sr[...], si[...], tr[...], ti[...]
    conv[...] = inverse(x_real * t_real - x_imag * t_imag, x_real * t_imag + x_imag * t_real, tables)


def middle_kernel(own, a, b, c, outer_t, conv, out, hidden_grad_t):
    total = (own[...].astype(jnp.float32) + a[...].astype(jnp.float32)) + (
        b[...].astype(jnp.float32) + c[...].astype(jnp.float32)
    )
    hidden_grad_t[...] = total
    out[:, :LANE_CH, :] = chunks(total * outer_t[...].astype(jnp.float32))
    out[:, LANE_CH:, :] = conv[...]


def second_kernel(got, gated, sr, si, tr, ti, *refs):
    tables, (out, outer_grad) = dict(zip(TABLES, refs)), refs[-2:]
    outer_grad[...] = gated[...]
    g_real, g_imag = forward(got[:, :LANE_CH, :], tables)
    t_real, t_imag = tr[...], ti[...]
    out[:, :LANE_CH, :] = inverse(
        t_real * g_real + t_imag * g_imag, t_real * g_imag - t_imag * g_real, tables
    )
    x_real, x_imag = sr[...], si[...]
    out[:, LANE_CH:, :] = inverse(
        x_real * g_real + x_imag * g_imag, x_real * g_imag - x_imag * g_real, tables
    )


def gate_kernel(got, outer, hidden_grad_t, hidden, gated):
    mixed_pre = flat(got[:, LANE_CH:, :]).astype(jnp.float32)
    hidden[...] = bf16(outer[...].astype(jnp.float32) * mixed_pre.T)
    gated[...] = bf16((hidden_grad_t[...] * mixed_pre).T)


def final_kernel(got, inner, values, inner_grad, values_grad, taps_grad):
    total = flat(got[:, :LANE_CH, :]).astype(jnp.float32).T
    inner_grad[...] = bf16(total * values[...].astype(jnp.float32))
    values_grad[...] = bf16(total * inner[...].astype(jnp.float32))
    taps_grad[...] = flat(got[:, LANE_CH:, :]).astype(jnp.float32).T


def token_kernel(sent, hidden, out):
    out[...] = hidden[:16, :128]


def block_ids(where):
    row, core, turn = where[0], where[1], 2 * where[1] - 1
    near = [2 * (r & 3) + core for r in (row, row - turn, row + turn)]
    far = [2 * (r & 3) + 1 - core for r in (row, row + turn, row - turn)]
    return near + far, [2 * ((row + 2) & 3) + core, 2 * ((row + 2) & 3) + 1 - core]


def fetch_kernel(where, weight, token, sent, out, sems):
    copies = [
        pltpu.make_async_copy(weight.at[block], out.at[i], sems.at[i])
        for i, block in enumerate(block_ids(where)[0])
    ]
    for copy in copies:
        copy.start()
    for copy in copies:
        copy.wait()


def near_mixed_kernel(where, weight, kept, *refs):
    parts, (out, rest, sems) = refs[:6], refs[6:]
    copies = [
        pltpu.make_async_copy(weight.at[block], rest.at[i], sems.at[i])
        for i, block in enumerate(block_ids(where)[1])
    ]

    @pl.when(where[0] >= 0)
    def _():
        for copy in copies:
            copy.start()

    @pl.when(where[0] >= 0)
    def _():
        for c in range(0, COLUMNS, 256):
            columns = slice(c, c + 256)
            total = dot(parts[0][...], kept[0, :, columns])
            for i in range(1, 6):
                total += dot(parts[i][...], kept[i, :, columns])
            out[:, columns] = total

    for copy in copies:
        copy.wait()


def far_mixed_kernel(rest, near, far, base, out):
    for c in range(0, COLUMNS, 256):
        columns = slice(c, c + 256)
        total = base[:, columns] + dot(near[...], rest[0, :, columns])
        out[:, columns] = bf16(total + dot(far[...], rest[1, :, columns]))


def shape(dims, dtype):
    return jax.ShapeDtypeStruct(dims, dtype)


def inside(dims, dtype):
    return pltpu.VMEM(dims, dtype)


def outside(dims, dtype):
    return pltpu.HBM(dims, dtype)


VMEM = pl.BlockSpec(memory_space=pltpu.VMEM)
HBM = pl.BlockSpec(memory_space=pltpu.HBM)
SMEM = pl.BlockSpec(memory_space=pltpu.SMEM)


def local(kernel, outs, *args, limit=16, specs=None, out_specs=None, scratch=(), hold=(), cost=0.0):
    n = len(args)

    def body(*refs):
        kernel(*refs[:n], *refs[n + len(hold) :])

    return pl.pallas_call(
        body,
        out_shape=outs,
        in_specs=list(specs or [VMEM] * n) + [VMEM] * len(hold),
        out_specs=out_specs or tuple(VMEM for _ in outs),
        scratch_shapes=scratch,
        compiler_params=pltpu.CompilerParams(vmem_limit_bytes=limit << 20),
        cost_estimate=pl.CostEstimate(flops=int(cost * 1.15e9), bytes_accessed=1 << 16, transcendentals=0),
    )(*args, *map(near_memory, hold))


def far_memory(a):
    return pltpu.with_memory_space_constraint(a, pltpu.HBM)


def near_memory(a):
    return pltpu.with_memory_space_constraint(a, pltpu.VMEM)


def project(first, count, where, weight, grad, cost):
    return local(
        lambda *refs: project_kernel(first, *refs),
        (inside((count, WIDTH, ROWS), jnp.bfloat16),),
        where,
        weight,
        grad,
        specs=[SMEM, HBM, VMEM],
        scratch=[pltpu.VMEM((count, WIDTH, COLUMNS), jnp.bfloat16), pltpu.SemaphoreType.DMA((count,))],
        cost=cost,
    )[0]


def exchange(a):
    return lax.all_to_all(a, "seq", split_axis=0, concat_axis=0, tiled=True)


def to_partner(a):
    return lax.ppermute(a, "ch", [(i, i ^ 1) for i in range(8)])


def along(a, way):
    pairs = [(2 * y + c, 2 * ((y + way * (1 - 2 * c)) % 4) + c) for y in range(4) for c in range(2)]
    return lax.ppermute(a, "ch", pairs)


def shifted(a, rows):
    return lax.ppermute(a, "ch", [(i, (i + 2 * rows) % 8) for i in range(8)])


def on_device(outer_gate, inner_gate, values, filter_taps, skip_scale, out_weight, out_grad):
    tables = [far_memory(transform_tables()[i]) for i in (0, 3, 4, 2, 1)]
    me = lax.axis_index("ch").astype(jnp.int32)
    row, core = me // 2, me % 2
    near_half, far_half = jnp.stack([row, core]), jnp.stack([row, 1 - core])
    block = (WIDTH, ROWS)
    block_row = (ROWS, WIDTH)
    sending = (SEQ_PARTS, 2 * LANE_CH, ROWS)
    weight = far_memory(out_weight.reshape(8, WIDTH, COLUMNS))

    skip = jnp.where(lax.axis_index("seq") == 0, skip_scale, 0.0).reshape(1, WIDTH)
    sent = local(
        prepare_kernel,
        (inside(sending, jnp.bfloat16),),
        *map(far_memory, (inner_gate, values, filter_taps)),
        skip,
        limit=8,
        cost=COSTS[8],
    )[0]
    sent, far_half, near_half = lax.optimization_barrier((sent, far_half, near_half))
    got = near_memory(exchange(sent))
    given = project(2, 4, far_half, weight, out_grad, COSTS[0])
    given, near_half = lax.optimization_barrier((given, near_half))
    kept = project(2, 1, near_half, weight, out_grad, COSTS[1])
    other = near_memory(to_partner(given))
    across = local(
        lambda *refs: add_kernel(0, *refs), (inside(block, jnp.bfloat16),), kept, other
    )[0]
    across, near_half = lax.optimization_barrier((across, near_half))
    kept = project(3, 3, near_half, weight, out_grad, COSTS[1])
    back, own, ahead = local(
        lambda *refs: add_kernel(1, *refs),
        (inside(block, jnp.bfloat16), outside(block, jnp.bfloat16), inside(block, jnp.bfloat16)),
        kept,
        other,
    )
    across = near_memory(shifted(across, 2))
    sums = [across, shifted(ahead, 1), shifted(back, 3)]

    spectrum = inside((SLOTS * LANE_CH, ROWS), jnp.float32)
    *kept, own = local(
        first_kernel,
        (
            *(spectrum,) * 4,
            *(inside(t.shape, t.dtype) for t in tables),
            inside(block, jnp.bfloat16),
        ),
        near_half,
        got,
        *tables,
        far_memory(own),
        specs=[SMEM, VMEM] + [HBM] * (len(tables) + 1),
        scratch=[
            pltpu.SemaphoreType.DMA((len(tables) + 1,)),
            pltpu.VMEM((4, 2 * LINES, ROWS), jnp.float32),
        ],
        hold=(across,),
        cost=COSTS[6],
    )
    conv, outer_t = local(
        conv_kernel,
        (inside((SEQ_PARTS, LANE_CH, ROWS), jnp.bfloat16), inside(block, jnp.bfloat16)),
        *map(near_memory, kept),
        outer_gate,
        cost=COSTS[7],
    )
    sent, hidden_grad_t = local(
        middle_kernel,
        (inside(sending, jnp.bfloat16), inside(block, jnp.float32)),
        near_memory(own),
        *sums,
        outer_t,
        conv,
        hold=kept,
    )
    got = near_memory(exchange(sent))
    hidden, gated = local(
        gate_kernel,
        (inside(block_row, jnp.bfloat16), inside(block_row, jnp.bfloat16)),
        got,
        outer_gate,
        near_memory(hidden_grad_t),
        hold=kept,
    )
    sent, outer_grad = local(
        second_kernel,
        (outside(sending, jnp.bfloat16), outside(block_row, jnp.bfloat16)),
        got,
        *map(near_memory, (gated, *kept)),
        hold=(hidden,),
    )
    returned = near_memory(exchange(sent))
    before = along(hidden, 1)
    if LATE:
        after = None
    else:
        after = along(hidden, -1)
    token = local(
        token_kernel,
        (inside((16, 128), jnp.bfloat16),),
        far_memory(sent),
        hidden,
        specs=[HBM, VMEM],
    )[0]
    passed, turned_back, token = lax.optimization_barrier((before, hidden, token))
    if LATE:
        after = along(turned_back, -1)
    kept_weight = local(
        fetch_kernel,
        (inside((6, WIDTH, COLUMNS), weight.dtype),),
        near_half,
        weight,
        token,
        far_memory(sent),
        specs=[SMEM, HBM, VMEM, HBM],
        scratch=[pltpu.SemaphoreType.DMA((6,))],
        cost=COSTS[2],
    )[0]
    across = along(passed, 1)
    near = [hidden, after, before]
    far = [to_partner(a) for a in near]
    part, rest = local(
        near_mixed_kernel,
        (inside((ROWS, COLUMNS), jnp.float32), inside((2, WIDTH, COLUMNS), weight.dtype)),
        near_half,
        weight,
        kept_weight,
        *near,
        *far,
        specs=[SMEM, HBM] + [VMEM] * 7,
        scratch=[pltpu.SemaphoreType.DMA((2,))],
        cost=COSTS[3],
    )
    mixed = local(
        far_mixed_kernel,
        (outside((ROWS, COLUMNS), jnp.bfloat16),),
        rest,
        across,
        to_partner(across),
        part,
        cost=COSTS[4],
    )[0]
    inner_grad, values_grad, taps_grad = local(
        final_kernel,
        (
            outside(block_row, jnp.bfloat16),
            outside(block_row, jnp.bfloat16),
            outside(block_row, jnp.float32),
        ),
        returned,
        inner_gate,
        values,
    )
    return (mixed, outer_grad, inner_grad, values_grad, taps_grad)


def solution(mesh):
    placed = (
        P("seq", "ch"),
        P("seq", "ch"),
        P("seq", "ch"),
        P("seq", "ch"),
        P("ch"),
        P(None, "ch"),
        P("seq", "ch"),
    )
    return jax.shard_map(
        on_device,
        mesh=mesh,
        in_specs=placed,
        out_specs=(P("seq", "ch"), P("seq", "ch"), P("seq", "ch"), P("seq", "ch"), P("seq", "ch")),
        check_vma=False,
    )
```
